32 devices in a mesh: space: 4 (over z), node: 4 (over x, core), tm: 2 (over y).
Axes of the slice: x: 2, y: 2, z: 4, core: 2. Of those that a mesh axis runs over, the one named last changes fastest.
Arguments:
- start_old: float32 [2, 32, 128, 256], P('tm', 'space'), may hold values from -4 to 4
- nodes_old: float32 [2, 4, 32, 128, 256], P('tm', 'node', 'space'), may hold values from -4 to 4
Outputs:
- nodes_new: float32 [2, 4, 32, 128, 256], P('tm', 'node', 'space')
- end_new: float32 [2, 32, 128, 256], P('tm', 'space')
The draws below stay inside these ranges and needn't reach their ends.
All inputs are finite; a program needn't handle non-finite values.
Results may differ from the reference program's by a relative error of at most 0.00002.
Values sent between devices are 32-bit elements; how exact they have to be, the bound alone decides.
No kernel may reach another device: no remote copies, remote signals or barrier semaphores. Data moves between devices by JAX's collectives and lax.ppermute only.
A program may use at most 64 MiB of HBM per device.

```python
import jax
import jax.numpy as jnp

NX = 256
NY = 128
NODES = 4
PASSES = 4
SLICES = 2
NZ = 32


def levels(key, dims, cuts, low, top_value):
    loudness, own = 1.0, jax.random.fold_in(key, 6)
    for axis_at, shards_of in cuts:
        draws = jnp.exp(jax.random.uniform(jax.random.fold_in(own, axis_at), (shards_of,), jnp.float32, low / len(cuts), top_value / len(cuts)))
        loudness = loudness * jnp.repeat(draws, dims[axis_at] // shards_of).reshape([-1 if axis == axis_at else 1 for axis in range(len(dims))])
    return loudness


def centred(own_key, dims, deviation, limit, split=(), dtype=jnp.bfloat16):
    entries = deviation * jax.random.normal(own_key, dims, jnp.float32)
    if split:
        entries = entries * levels(own_key, dims, split, -0.22, 0.18)
    return jnp.clip(entries, -limit, limit).astype(dtype)


def setup_inputs(seed: int = 0) -> dict:
    key_list = jax.random.split(jax.random.key(seed), 3)
    return {
        "start_old": centred(key_list[0], (SLICES, NZ, NY, NX), 1.0, 4.0, ((0, 2), (1, 4)), jnp.float32),
        "nodes_old": centred(key_list[1], (SLICES, NODES, NZ, NY, NX), 1.0, 4.0, ((0, 2), (1, 4), (2, 4)), jnp.float32),
    }


time_step = 0.25
diffusion = 4.0
reaction = 1.0


def collocation(count):
    points = [-0.8611363115940526, -0.3399810435848563, 0.3399810435848563, 0.8611363115940526]
    raw_weights = [0.3478548451374538, 0.6521451548625461, 0.6521451548625461, 0.3478548451374538]
    node_times = [(point + 1.0) / 2.0 for point in points]
    quadrature = [[0.0 for column in range(count)] for target in range(count)]
    for source in range(count):
        coeffs = [1.0]
        scaling = 1.0
        for other in range(count):
            if other != source:
                other_time = node_times[other]
                shifted = [0.0] + coeffs
                for power in range(len(coeffs)):
                    shifted[power] = shifted[power] - other_time * coeffs[power]
                coeffs = shifted
                scaling = scaling * (node_times[source] - other_time)
        for target in range(count):
            target_time = node_times[target]
            integral = 0.0
            for power in range(len(coeffs)):
                integral = integral + coeffs[power] * target_time ** (power + 1) / (power + 1)
            quadrature[target][source] = integral / scaling
    return node_times, quadrature, [weight / 2.0 for weight in raw_weights]


def neighbour_sum(values):
    total = jnp.roll(values, -1, 0) + jnp.roll(values, 1, 0)
    total = total + jnp.roll(values, -1, 1) + jnp.roll(values, 1, 1)
    total = total + jnp.roll(values, -1, 2) + jnp.roll(values, 1, 2)
    return total


def forcing(values):
    laplace = neighbour_sum(values) - 6.0 * values
    return laplace, diffusion * laplace + reaction * (values - values * values * values)


def reference(start_old, nodes_old):
    node_times, quadrature, weights = collocation(NODES)
    all_nodes = []
    all_ends = []
    previous_end = start_old[0]
    for interval in range(SLICES):
        laplaces = []
        forces = []
        for source in range(NODES):
            laplace, force = forcing(nodes_old[interval, source])
            laplaces.append(laplace)
            forces.append(force)
        weighted = jnp.zeros_like(forces[0])
        for source in range(NODES):
            weighted = weighted + float(weights[source]) * forces[source]
        end_old = start_old[interval] + time_step * weighted
        begin_state = start_old[0] if interval == 0 else previous_end
        previous_end = end_old
        new_nodes = []
        for target in range(NODES):
            quad_sum = jnp.zeros_like(forces[0])
            for source in range(NODES):
                quad_sum = quad_sum + float(quadrature[target][source]) * forces[source]
            implicit = time_step * diffusion * float(node_times[target])
            right_side = begin_state + time_step * quad_sum - implicit * laplaces[target]
            iterate = nodes_old[interval, target]
            for step_index in range(PASSES):
                iterate = (right_side + implicit * neighbour_sum(iterate)) / (1.0 + 6.0 * implicit)
            new_nodes.append(iterate)
        weighted_new = jnp.zeros_like(forces[0])
        for source in range(NODES):
            weighted_new = weighted_new + float(weights[source]) * forcing(new_nodes[source])[1]
        all_ends.append(begin_state + time_step * weighted_new)
        all_nodes.append(jnp.stack(new_nodes))
    return jnp.stack(all_nodes), jnp.stack(all_ends)
```

```python
import functools

import jax
import jax.numpy as jnp
import numpy as np
from jax import lax
from jax.experimental import pallas as pl
from jax.experimental.pallas import tpu as pltpu
from jax.sharding import PartitionSpec as P

NODES = 4
PASSES = 4
DEPTH = PASSES + 1

time_step = 0.25
diffusion = 4.0
reaction = 1.0

F32 = jnp.float32


def collocation(count):
    points = [-0.8611363115940526, -0.3399810435848563, 0.3399810435848563, 0.8611363115940526]
    raw_weights = [0.3478548451374538, 0.6521451548625461, 0.6521451548625461, 0.3478548451374538]
    node_times = [(point + 1.0) / 2.0 for point in points]
    quadrature = [[0.0 for column in range(count)] for target in range(count)]
    for source in range(count):
        coeffs = [1.0]
        scaling = 1.0
        for other in range(count):
            if other != source:
                other_time = node_times[other]
                shifted = [0.0] + coeffs
                for power in range(len(coeffs)):
                    shifted[power] = shifted[power] - other_time * coeffs[power]
                coeffs = shifted
                scaling = scaling * (node_times[source] - other_time)
        for target in range(count):
            target_time = node_times[target]
            integral = 0.0
            for power in range(len(coeffs)):
                integral = integral + coeffs[power] * target_time ** (power + 1) / (power + 1)
            quadrature[target][source] = integral / scaling
    return (node_times, quadrature, [weight / 2.0 for weight in raw_weights])


LIN, CUB, WEIGHT, MIX, SCALE, FIRST, CORE, COUNT = 0, 8, 16, 20, 22, 24, 25, 26


def scalar_table():
    times, quad, weights = collocation(NODES)
    table = np.zeros((NODES, COUNT), np.float64)
    for node in range(NODES):
        sources = [node, node ^ 2, node ^ 1, node ^ 3]
        for place, target in enumerate([node, node ^ 2]):
            implicit = time_step * diffusion * times[target]
            for index, source in enumerate(sources):
                lin = time_step * diffusion * quad[target][source]
                table[node, LIN + 4 * place + index] = lin - (implicit if source == target else 0.0)
                table[node, CUB + 4 * place + index] = time_step * reaction * quad[target][source]
            table[node, MIX + place] = implicit / (1.0 + 6.0 * implicit)
            table[node, SCALE + place] = 1.0 / (1.0 + 6.0 * implicit)
        for index, source in enumerate(sources):
            table[node, WEIGHT + index] = weights[source]
        table[node, CORE] = node & 1
    return table.astype(np.float32)


def flat_sum(plane):
    rows, columns = plane.shape
    vertical = pltpu.roll(plane, 1, 0) + pltpu.roll(plane, rows - 1, 0)
    return vertical + (pltpu.roll(plane, 1, 1) + pltpu.roll(plane, columns - 1, 1))


def mixed(scalars, base, planes):
    own, across, beside, corner = (scalars[base + index] * plane for index, plane in enumerate(planes))
    return (own + across) + (beside + corner)


def joined(core, mine, other):
    return jnp.where(core, other, mine), jnp.where(core, mine, other)


def end_kernel(upper, scalars, own, across, beside, corner, start, out, total):
    shift = 3 if upper else 0
    half = out.shape[1]
    core = scalars[CORE] > 0.5

    def gathered(plane):
        return [ref[plane] for ref in (own, across, beside, corner)]

    for plane in range(5):
        total[plane] = mixed(scalars, WEIGHT, gathered(plane))
    for place in range(5):
        plane = place + 4 if upper else place - 1
        if plane in (-1, 8):
            value = (time_step * diffusion) * total[0 if plane < 0 else 4]
        else:
            middle = total[plane - shift]
            around = flat_sum(middle)
            if plane + 1 < 8:
                around = around + total[plane + 1 - shift]
            if plane > 0:
                around = around + total[plane - 1 - shift]
            states = gathered(plane - shift)
            local = mixed(scalars, WEIGHT, [state - state * state * state for state in states])
            force = diffusion * (around - 6.0 * middle) + reaction * local
            value = start[plane - shift] + time_step * force
        out[place] = jnp.where(core, value[half:], value[:half])


def sweep_kernel(scalars, *refs):
    names = ["own", "across_a", "across_b", "beside", "corner_a", "corner_b"]
    names += [f"{side}{part}_{who}" for side in ("low", "high") for part in "ab" for who in ("own", "across", "beside", "corner")]
    names += ["start", "start_low", "start_low_", "start_high", "start_high_"]
    names += [f"{kind}{end}" for kind in ("end_low", "end_high", "above_low", "below_high") for end in ("", "_")]
    names += ["out", "share", "x_own", "x_across", "y_own", "y_across", "r_own", "r_across", "begin"]
    r = dict(zip(names, refs, strict=True))
    slab = r["own"].shape[0]
    core = scalars[CORE] > 0.5
    first = scalars[FIRST]
    half = r["start_low"].shape[1]
    edge = DEPTH

    begin = r["begin"]

    def put(place, value_low, value_high):
        begin[place, :half] = value_low
        begin[place, half:] = value_high

    def both(name, index):
        return joined(core, r[name][index], r[name + "_"][index])

    def add(first_pair, second_pair):
        return first_pair[0] + second_pair[0], first_pair[1] + second_pair[1]

    for index in range(4):
        pair = add(both("start_low", index), both("below_high", index))
        if index == 3:
            pair = add(pair, both("end_low", 0))
        put(index, *pair)
        pair = add(both("start_high", index), both("above_low", index + 1))
        if index == 0:
            pair = add(pair, both("end_high", 4))
        put(index + 12, *pair)
        pair = both("end_low", index + 1)
        if index == 0:
            pair = add(pair, both("below_high", 4))
        mine = first * r["start"][index]
        put(index + 4, *add(pair, (mine[:half], mine[half:])))
        pair = both("end_high", index)
        if index == 3:
            pair = add(pair, both("above_low", 0))
        mine = first * r["start"][index + 4]
        put(index + 8, *add(pair, (mine[:half], mine[half:])))

    def pointwise(place, count, sources, offset):
        def body(index, carry):
            states = [source[offset[number] + index] for number, source in enumerate(sources)]
            local = [state - state * state * state for state in states]
            r["x_own"][place + index] = states[0]
            r["x_across"][place + index] = states[1]
            r["y_own"][place + index] = mixed(scalars, LIN, states)
            r["y_across"][place + index] = mixed(scalars, LIN + 4, states)
            r["r_own"][place + index] = mixed(scalars, CUB, local)
            r["r_across"][place + index] = mixed(scalars, CUB + 4, local)
            return carry

        lax.fori_loop(0, count, body, 0)

    who = ("own", "across", "beside", "corner")
    pointwise(0, 2, [r["lowb_" + name] for name in who], (0,) * 4)
    pointwise(2, 3, [r["lowa_" + name] for name in who], (0,) * 4)
    pointwise(edge, 5, [r["own"], r["across_a"], r["beside"], r["corner_a"]], (0,) * 4)
    pointwise(edge + 5, 3, [r["own"], r["across_b"], r["beside"], r["corner_b"]], (5, 0, 5, 0))
    pointwise(edge + slab, 3, [r["higha_" + name] for name in who], (0,) * 4)
    pointwise(edge + slab + 3, 2, [r["highb_" + name] for name in who], (0,) * 4)

    def grouped(low, high, group, step):
        count = (high - low) // group

        def body(index, carry):
            for member in range(group):
                step(low + index * group + member)
            return carry

        lax.fori_loop(0, count, body, 0)
        for place in range(low + count * group, high):
            step(place)

    def around(ref, place):
        return (ref[place + 1] + ref[place - 1]) + flat_sum(ref[place])

    def right(place):
        for index, name in enumerate(("own", "across")):
            potential = r["y_" + name]
            value = (around(potential, place) - 6.0 * potential[place]) + r["r_" + name][place]
            r["r_" + name][place] = scalars[SCALE + index] * (value + begin[place - 1])

    grouped(1, 2 * edge + slab - 1, 4, right)

    for step_index in range(PASSES):
        source, target = ("x_", "y_") if step_index % 2 == 0 else ("y_", "x_")

        def relax(place, source=source, target=target):
            for index, name in enumerate(("own", "across")):
                value = scalars[MIX + index] * around(r[source + name], place)
                r[target + name][place] = r["r_" + name][place] + value

        grouped(1 + step_index, 2 * edge + slab - 1 - step_index, 4, relax)

    final, spare = ("x_", "y_") if PASSES % 2 == 0 else ("y_", "x_")
    weights = (scalars[WEIGHT], scalars[WEIGHT + 1])

    def weigh(place):
        r[spare + "own"][place] = weights[0] * r[final + "own"][place] + weights[1] * r[final + "across"][place]

    grouped(edge - 1, edge + slab + 1, 5, weigh)

    def finish(place):
        total = r[spare + "own"]
        states = [r[final + name][place] for name in ("own", "across")]
        local = [state - state * state * state for state in states]
        force = diffusion * (around(total, place) - 6.0 * total[place])
        force = force + reaction * (weights[0] * local[0] + weights[1] * local[1])
        r["out"][place - edge] = states[0]
        r["share"][place - edge] = time_step * force + 0.5 * begin[place - 1]

    grouped(edge, edge + slab, 4, finish)


def in_vmem(count):
    return [pl.BlockSpec(memory_space=pltpu.SMEM)] + [pl.BlockSpec(memory_space=pltpu.VMEM)] * count


def end_call(upper, scalars, sources, start):
    planes, rows, columns = sources[0].shape
    return pl.pallas_call(
        functools.partial(end_kernel, upper),
        out_shape=jax.ShapeDtypeStruct((5, rows // 2, columns), F32),
        in_specs=in_vmem(5),
        out_specs=pl.BlockSpec(memory_space=pltpu.VMEM),
        scratch_shapes=[pltpu.VMEM((5, rows, columns), F32)],
        compiler_params=pltpu.CompilerParams(vmem_limit_bytes=16 << 20),
        cost_estimate=pl.CostEstimate(flops=5 * rows * columns * 40, bytes_accessed=30 * rows * columns * 4, transcendentals=0),
    )(scalars, *sources, start)


def sweep_call(scalars, operands, shape):
    slab, rows, columns = shape
    wide = pltpu.VMEM((slab + 2 * DEPTH, rows, columns), F32)
    return pl.pallas_call(
        sweep_kernel,
        out_shape=[jax.ShapeDtypeStruct(shape, F32)] * 2,
        in_specs=in_vmem(len(operands)),
        out_specs=[pl.BlockSpec(memory_space=pltpu.VMEM)] * 2,
        scratch_shapes=[wide] * 6 + [pltpu.VMEM((slab + 2 * DEPTH - 2, rows, columns), F32)],
        compiler_params=pltpu.CompilerParams(vmem_limit_bytes=40 << 20),
        cost_estimate=pl.CostEstimate(flops=200 * rows * columns * 20, bytes_accessed=300 * rows * columns * 4, transcendentals=0),
    )(scalars, *operands)


def on_device(start_old, nodes_old):
    slabs, slices = lax.axis_size("space"), lax.axis_size("tm")
    node_index = lax.axis_index("node")
    slice_index = lax.axis_index("tm")
    state, start = nodes_old[0, 0], start_old[0]
    slab, rows, columns = state.shape
    half = rows // 2
    core = lax.rem(node_index, 2)
    scalars = jnp.asarray(scalar_table())[node_index]
    scalars = scalars.at[FIRST].set((slice_index == 0).astype(F32))

    def across(array):
        return lax.ppermute(array, "node", [(node, node ^ 2) for node in range(NODES)])

    def beside(array):
        return lax.ppermute(array, "node", [(node, node ^ 1) for node in range(NODES)])

    def along(array, by):
        return lax.ppermute(array, "space", [(slab_, (slab_ + by) % slabs) for slab_ in range(slabs)])

    def onward(array, by, source=None):
        if source is None:
            steps = [(slice_, slice_ + 1) for slice_ in range(slices - 1)]
        else:
            steps = [(0, 0)]
        pairs = [
            (slab_ * slices + here, ((slab_ + by) % slabs) * slices + there) for slab_ in range(slabs) for here, there in steps
        ]
        return lax.ppermute(array, ("space", "tm"), pairs)

    across_a = across(state[:5])
    across_b = across(state[5:])
    low_a, high_a = along(state[5:], 1), along(state[:3], -1)
    low_b, high_b = along(state[3:5], 1), along(state[3:5], -1)
    own_beside = beside(state)
    halo = {"lowa": low_a, "lowb": low_b, "higha": high_a, "highb": high_b}
    far = {name: across(array) for name, array in halo.items()}

    corner_a, corner_b = beside(across_a), beside(across_b)
    middle = jnp.concatenate([across_a[3:], across_b], axis=0)
    corner_middle = jnp.concatenate([corner_a[3:], corner_b], axis=0)
    end_low = end_call(False, scalars, [state[:5], across_a, own_beside[:5], corner_a], start[:5])
    end_high = end_call(True, scalars, [state[3:], middle, own_beside[3:], corner_middle], start[3:])
    got = {
        "end_low": onward(end_low, 0),
        "end_high": onward(end_high, 0),
        "above_low": onward(end_low, -1),
        "below_high": onward(end_high, 1),
    }
    mine = lax.dynamic_slice_in_dim(start, core * half, half, axis=1)
    start_low = onward(mine[4:], 1, source=0)
    start_high = onward(mine[:4], -1, source=0)

    operands = [state, across_a, across_b, own_beside, corner_a, corner_b]
    for name in ("lowa", "lowb", "higha", "highb"):
        operands += [halo[name], far[name], beside(halo[name]), beside(far[name])]
    operands += [start, start_low, beside(start_low), start_high, beside(start_high)]
    for name in ("end_low", "end_high", "above_low", "below_high"):
        operands += [got[name], beside(got[name])]
    state_new, share = sweep_call(scalars, operands, state.shape)
    end_new = share + beside(share)
    return (state_new[None, None], end_new[None])


def solution(mesh):
    return jax.shard_map(
        on_device,
        mesh=mesh,
        in_specs=(P("tm", "space", None, None), P("tm", "node", "space", None, None)),
        out_specs=(P("tm", "node", "space", None, None), P("tm", "space", None, None)),
        check_vma=False,
    )
```

```python
import functools

import jax
import jax.numpy as jnp
import numpy as np
from jax import lax
from jax.experimental import pallas as pl
from jax.experimental.pallas import tpu as pltpu
from jax.sharding import PartitionSpec as P

NODES = 4
PASSES = 4
DEPTH = PASSES + 1

time_step = 0.25
diffusion = 4.0
reaction = 1.0

F32 = jnp.float32


def collocation(count):
    points = [-0.8611363115940526, -0.3399810435848563, 0.3399810435848563, 0.8611363115940526]
    raw_weights = [0.3478548451374538, 0.6521451548625461, 0.6521451548625461, 0.3478548451374538]
    node_times = [(point + 1.0) / 2.0 for point in points]
    quadrature = [[0.0 for column in range(count)] for target in range(count)]
    for source in range(count):
        coeffs = [1.0]
        scaling = 1.0
        for other in range(count):
            if other != source:
                other_time = node_times[other]
                shifted = [0.0] + coeffs
                for power in range(len(coeffs)):
                    shifted[power] = shifted[power] - other_time * coeffs[power]
                coeffs = shifted
                scaling = scaling * (node_times[source] - other_time)
        for target in range(count):
            target_time = node_times[target]
            integral = 0.0
            for power in range(len(coeffs)):
                integral = integral + coeffs[power] * target_time ** (power + 1) / (power + 1)
            quadrature[target][source] = integral / scaling
    return (node_times, quadrature, [weight / 2.0 for weight in raw_weights])


LIN, CUB, WEIGHT, MIX, SCALE, FIRST, CORE, COUNT = 0, 8, 16, 20, 22, 24, 25, 26


def scalar_table():
    times, quad, weights = collocation(NODES)
    table = np.zeros((NODES, COUNT), np.float64)
    for node in range(NODES):
        sources = [node, node ^ 2, node ^ 1, node ^ 3]
        for place, target in enumerate([node, node ^ 2]):
            implicit = time_step * diffusion * times[target]
            for index, source in enumerate(sources):
                lin = time_step * diffusion * quad[target][source]
                table[node, LIN + 4 * place + index] = lin - (implicit if source == target else 0.0)
                table[node, CUB + 4 * place + index] = time_step * reaction * quad[target][source]
            table[node, MIX + place] = implicit / (1.0 + 6.0 * implicit)
            table[node, SCALE + place] = 1.0 / (1.0 + 6.0 * implicit)
        for index, source in enumerate(sources):
            table[node, WEIGHT + index] = weights[source]
        table[node, CORE] = node & 1
    return table.astype(np.float32)


def flat_sum(plane):
    rows, columns = plane.shape
    vertical = pltpu.roll(plane, 1, 0) + pltpu.roll(plane, rows - 1, 0)
    return vertical + (pltpu.roll(plane, 1, 1) + pltpu.roll(plane, columns - 1, 1))


def mixed(scalars, base, planes):
    own, across, beside, corner = (scalars[base + index] * plane for index, plane in enumerate(planes))
    return (own + across) + (beside + corner)


def cubed(state):
    return state - state * state * state


def around(ref, place):
    return (ref[place + 1] + ref[place - 1]) + flat_sum(ref[place])


def grouped(low, high, group, step):
    count = (high - low) // group

    def body(index, carry):
        for member in range(group):
            step(low + index * group + member)
        return carry

    if count > 1:
        lax.fori_loop(0, count, body, 0)
    elif count:
        body(0, 0)
    for place in range(low + count * group, high):
        step(place)


def send_kernel(scalars, own, beside, start, halo_a, halo_b, halo_start):
    upwards = scalars[CORE] < 0.5
    slab = own.shape[0]

    def copy(first_a, first_start):
        for index in range(3):
            halo_a[index] = own[first_a + index]
            halo_a[index + 3] = beside[first_a + index]
        for index in range(4):
            halo_start[index] = start[first_start + index]

    pl.when(upwards)(lambda: copy(slab - 3, slab - 4))
    pl.when(jnp.logical_not(upwards))(lambda: copy(0, 0))
    for index in range(2):
        halo_b[index] = own[3 + index]
        halo_b[index + 2] = beside[3 + index]


def end_kernel(scalars, own, beside, across, corner, start, low, high, total):
    slab = own.shape[0]

    def states_at(plane):
        return own[plane], across[plane], beside[plane], corner[plane]

    total[0] = jnp.zeros_like(total[0])
    total[slab + 1] = jnp.zeros_like(total[0])

    def weigh(plane):
        total[plane + 1] = mixed(scalars, WEIGHT, states_at(plane))

    def force(plane, out, place):
        laplace = around(total, plane + 1) - 6.0 * total[plane + 1]
        local = mixed(scalars, WEIGHT, [cubed(state) for state in states_at(plane)])
        out[place] = start[plane] + time_step * (diffusion * laplace + reaction * local)

    grouped(0, slab, 4, weigh)
    grouped(0, 4, 4, lambda plane: force(plane, low, plane + 1))
    grouped(4, 8, 4, lambda plane: force(plane, high, plane - 4))
    low[0] = (time_step * diffusion) * total[1]
    high[4] = (time_step * diffusion) * total[slab]


def last_kernel(
    scalars, start, start_near, start_far, low_near, low_far, high_near, high_far, part_own, part_across,
    out, share, begin, once, twice, last_own, last_across, total,
):
    first = scalars[FIRST]
    upwards = scalars[CORE] < 0.5
    slab = out.shape[0]

    def assemble(start_low, start_high, end_low, above_low, end_high, below_high):
        for index in range(4):
            value = start_low[index] + below_high[index]
            begin[index] = value + end_low[0] if index == 3 else value
            value = start_high[index] + above_low[index + 1]
            begin[index + 12] = value + end_high[4] if index == 0 else value
            value = first * start[index] + end_low[index + 1]
            begin[index + 4] = value + below_high[4] if index == 0 else value
            value = first * start[index + 4] + end_high[index]
            begin[index + 8] = value + above_low[0] if index == 3 else value

    pl.when(upwards)(lambda: assemble(start_near, start_far, low_near, low_far, high_near, high_far))
    pl.when(jnp.logical_not(upwards))(lambda: assemble(start_far, start_near, low_far, low_near, high_far, high_near))

    def first_power(place):
        once[place] = around(begin, place)

    def second_power(place):
        twice[place] = around(once, place)

    weights = (scalars[WEIGHT], scalars[WEIGHT + 1])
    last, part = (last_own, last_across), (part_own, part_across)

    def combine(place):
        thrice = around(twice, place)
        for target in range(2):
            mix = scalars[MIX + target]
            value = begin[place] + mix * (once[place] + mix * (twice[place] + mix * thrice))
            last[target][place - 3] = part[target][place - 3] + scalars[SCALE + target] * value
        total[place - 3] = weights[0] * last_own[place - 3] + weights[1] * last_across[place - 3]

    def finish(place):
        states = (last_own[place], last_across[place])
        force = diffusion * (around(total, place) - 6.0 * total[place])
        force = force + reaction * (weights[0] * cubed(states[0]) + weights[1] * cubed(states[1]))
        out[place - 1] = states[0]
        share[place - 1] = time_step * force + 0.5 * begin[place + 3]

    grouped(1, 15, 7, first_power)
    grouped(2, 14, 6, second_power)
    grouped(3, 13, 5, combine)
    grouped(1, slab + 1, 4, finish)


EDGE_V, EDGE_R, EDGE_RIGHT, EDGE_1, EDGE_2, EDGE_3, EDGE_COUNT = 0, 4, 6, 12, 16, 20, 24


def inner_kernel(
    scalars, own, beside, across, corner, near, far, across_near, across_far,
    edge_own, edge_across, middle_own, middle_across, x_own, x_across, y_own, y_across, r_own, r_across,
):
    x, y, r = (x_own, x_across), (y_own, y_across), (r_own, r_across)
    edge, middle = (edge_own, edge_across), (middle_own, middle_across)

    def pointwise(place, count, sources, offsets):
        def step(index):
            states = [source[offset + index] for source, offset in zip(sources, offsets)]
            local = [cubed(state) for state in states]
            for target in range(2):
                x[target][place + index] = states[target]
                y[target][place + index] = mixed(scalars, LIN + 4 * target, states)
                r[target][place + index] = mixed(scalars, CUB + 4 * target, local)

        grouped(0, count, 2, step)

    upwards = scalars[CORE] < 0.5

    def halos(near_place, far_place):
        pointwise(near_place, 3, (near, across_near, near, across_near), (0, 0, 3, 3))
        pointwise(far_place, 3, (far, across_far, far, across_far), (3, 3, 0, 0))

    pl.when(upwards)(lambda: halos(2, 13))
    pl.when(jnp.logical_not(upwards))(lambda: halos(13, 2))
    pointwise(5, 8, (own, across, beside, corner), (0, 0, 0, 0))

    def keep(source, base, planes):
        for target in range(2):
            for index, plane in enumerate(planes):
                edge[target][base + index] = source[target][plane + 5]

    def right(place):
        for target in range(2):
            value = (around(y[target], place) - 6.0 * y[target][place]) + r[target][place]
            r[target][place] = scalars[SCALE + target] * value

    grouped(3, 15, 4, right)
    keep(y, EDGE_V, (-3, -2, 9, 10))
    keep(r, EDGE_R, (-3, 10))
    keep(r, EDGE_RIGHT, (-2, -1, 0, 7, 8, 9))

    def passed(source, sink, shift=0):
        def step(place):
            for target in range(2):
                value = scalars[MIX + target] * around(source[target], place)
                sink[target][place - shift] = r[target][place] + value

        return step

    grouped(3, 15, 4, passed(x, y))
    keep(y, EDGE_1, (-2, -1, 8, 9))
    grouped(4, 14, 5, passed(y, x))
    keep(x, EDGE_2, (-1, 0, 7, 8))
    grouped(5, 13, 4, passed(x, y))
    keep(y, EDGE_3, (0, 1, 6, 7))
    grouped(6, 12, 3, passed(y, middle, 6))


def outer_kernel(
    scalars, near_a, far_a, across_near_a, across_far_a, near_b, far_b, across_near_b, across_far_b,
    edge_own, edge_across, middle_own, middle_across, part_own, part_across, x0, v, right, x1, x2, x3,
):
    upwards = scalars[CORE] < 0.5
    edge, middle, part = (edge_own, edge_across), (middle_own, middle_across), (part_own, part_across)
    corners = [(target, end) for target in range(2) for end in range(2)]

    def outermost(end, a, across_a, b, across_b, offset_a, offset_b):
        for q in (5, 4, 3, 2):
            index = {0: {5: 0, 4: 1, 3: 0, 2: 1}, 1: {5: 1, 4: 0, 3: 2, 2: 1}}[end][q]
            if q >= 4:
                pair, offset, other = (b, across_b), offset_b, 2 - offset_b
            else:
                pair, offset, other = (a, across_a), offset_a, 3 - offset_a
            states = [ref[offset + index] for ref in pair]
            for target in range(2):
                x0[target, end, 5 - q] = states[target]
            if q >= 4:
                states += [ref[other + index] for ref in pair]
                for target in range(2):
                    v[target, end, 5 - q] = mixed(scalars, LIN + 4 * target, states)
                    if q == 4:
                        right[target, end, 0] = mixed(scalars, CUB + 4 * target, [cubed(state) for state in states])

    def ends(near_end, far_end):
        outermost(near_end, near_a, across_near_a, near_b, across_near_b, 0, 0)
        outermost(far_end, far_a, across_far_a, far_b, across_far_b, 3, 2)

    pl.when(upwards)(lambda: ends(0, 1))
    pl.when(jnp.logical_not(upwards))(lambda: ends(1, 0))

    def kept(target, end, base, count, q_order):
        return edge[target][base + (q_order if end == 0 else 2 * count - 1 - q_order)]

    def laplacian(outside, centre, inside):
        return ((outside + inside) + flat_sum(centre)) - 6.0 * centre

    def relaxed(target, base, outside, centre, inside):
        return base + scalars[MIX + target] * ((outside + inside) + flat_sum(centre))

    for target, end in corners:
        scale = scalars[SCALE + target]
        v3, v2 = (kept(target, end, EDGE_V, 2, order) for order in range(2))
        value = laplacian(v[target, end, 0], v[target, end, 1], v3) + right[target, end, 0]
        right[target, end, 0] = scale * value
        right[target, end, 1] = scale * (laplacian(v[target, end, 1], v3, v2) + kept(target, end, EDGE_R, 1, 0))
    for target, end in corners:
        for index in range(2):
            x1[target, end, index] = relaxed(
                target, right[target, end, index], x0[target, end, index], x0[target, end, index + 1], x0[target, end, index + 2]
            )
    for target, end in corners:
        near2, near1 = (kept(target, end, EDGE_1, 2, order) for order in range(2))
        right2 = kept(target, end, EDGE_RIGHT, 3, 0)
        x2[target, end, 0] = relaxed(target, right[target, end, 1], x1[target, end, 0], x1[target, end, 1], near2)
        x2[target, end, 1] = relaxed(target, right2, x1[target, end, 1], near2, near1)
    for target, end in corners:
        near1, near0 = (kept(target, end, EDGE_2, 2, order) for order in range(2))
        right2, right1 = (kept(target, end, EDGE_RIGHT, 3, order) for order in range(2))
        x3[target, end, 0] = relaxed(target, right2, x2[target, end, 0], x2[target, end, 1], near1)
        x3[target, end, 1] = relaxed(target, right1, x2[target, end, 1], near1, near0)
    for target, end in corners:
        near0, inside = (kept(target, end, EDGE_3, 2, order) for order in range(2))
        right1, right0 = (kept(target, end, EDGE_RIGHT, 3, order) for order in (1, 2))
        place1, place0 = (0, 1) if end == 0 else (9, 8)
        part[target][place1] = relaxed(target, right1, x3[target, end, 0], x3[target, end, 1], near0)
        part[target][place0] = relaxed(target, right0, x3[target, end, 1], near0, inside)
    for target in range(2):
        for index in range(6):
            part[target][index + 2] = middle[target][index]


def call(kernel, scalars, operands, outs, scratch, limit):
    return pl.pallas_call(
        kernel,
        out_shape=[jax.ShapeDtypeStruct(shape, F32) for shape in outs],
        in_specs=[pl.BlockSpec(memory_space=pltpu.SMEM)] + [pl.BlockSpec(memory_space=pltpu.VMEM)] * len(operands),
        out_specs=[pl.BlockSpec(memory_space=pltpu.VMEM)] * len(outs),
        scratch_shapes=[pltpu.VMEM(shape, F32) for shape in scratch],
        compiler_params=pltpu.CompilerParams(vmem_limit_bytes=limit << 20),
        cost_estimate=pl.CostEstimate(flops=1000, bytes_accessed=1000, transcendentals=0),
    )(scalars, *operands)


def on_device(start_old, nodes_old):
    slabs, slices = lax.axis_size("space"), lax.axis_size("tm")
    node_index = lax.axis_index("node")
    slice_index = lax.axis_index("tm")
    state, start = nodes_old[0, 0], start_old[0]
    slab, rows, columns = state.shape
    scalars = jnp.asarray(scalar_table())[node_index]
    scalars = scalars.at[FIRST].set((slice_index == 0).astype(F32))

    def after(array, other):
        return lax.optimization_barrier((array, other))[0]

    def planes(*lead):
        return (*lead, rows, columns)

    def across(array):
        return lax.ppermute(array, "node", [(node, node ^ 2) for node in range(NODES)])

    def beside(array):
        return lax.ppermute(array, "node", [(node, node ^ 1) for node in range(NODES)])

    def place(slab_, node, slice_):
        return ((slab_ % slabs) * NODES + node) * slices + slice_

    def spread(array, steps, by):
        pairs = [
            (place(slab_, node, here), place(slab_ + by[node % 2], node, there))
            for slab_ in range(slabs) for node in range(NODES) for here, there in steps
        ]
        return lax.ppermute(array, ("space", "node", "tm"), pairs)

    same = [(slice_, slice_) for slice_ in range(slices)]
    onward = [(slice_, slice_ + 1) for slice_ in range(slices - 1)]

    beside_state = beside(state)
    across_state = across(state)
    halo_a, halo_b, halo_start = call(
        send_kernel, scalars, [state, beside_state, start], [planes(6), planes(4), planes(4)], [], 16
    )
    near_a = spread(halo_a, same, (1, -1))
    near_b = spread(halo_b, same, (1, -1))

    corner_state = beside(after(across_state, halo_a))
    sources = [state, beside_state, across_state, corner_state]
    end_low, end_high = call(end_kernel, scalars, [*sources, start], [planes(5)] * 2, [planes(slab + 2)], 16)
    low_near = spread(end_low, onward, (0, -1))
    high_near = spread(end_high, onward, (0, 1))

    across_near_a = across(near_a)
    far_a = beside(after(near_a, end_low))
    across_near_b = across(near_b)
    start_near = spread(after(halo_start, near_b), [(0, 0)], (1, -1))
    across_far_a = beside(across_near_a)

    wide = planes(slab + 2 * DEPTH)
    edge_own, edge_across, middle_own, middle_across = call(
        inner_kernel, scalars, [*sources, near_a, far_a, across_near_a, across_far_a],
        [planes(EDGE_COUNT)] * 2 + [planes(slab - 2)] * 2, [wide] * 6, 36,
    )
    far_b = beside(near_b)
    across_far_b = beside(after(across_near_b, edge_own))
    part_own, part_across = call(
        outer_kernel, scalars,
        [
            near_a, far_a, across_near_a, across_far_a, near_b, far_b, across_near_b, across_far_b,
            edge_own, edge_across, middle_own, middle_across,
        ],
        [planes(slab + 2)] * 2, [planes(2, 2, 4)] + [planes(2, 2, 2)] * 5, 24,
    )
    high_far = beside(after(high_near, edge_own))
    state_new, share = call(
        last_kernel, scalars,
        [start, start_near, beside(start_near), low_near, beside(low_near), high_near, high_far, part_own, part_across],
        [planes(slab)] * 2, [planes(slab + 8)] * 3 + [planes(slab + 2)] * 3, 24,
    )
    end_new = share + beside(share)
    return (state_new[None, None], end_new[None])


def solution(mesh):
    return jax.shard_map(
        on_device,
        mesh=mesh,
        in_specs=(P("tm", "space", None, None), P("tm", "node", "space", None, None)),
        out_specs=(P("tm", "node", "space", None, None), P("tm", "space", None, None)),
        check_vma=False,
    )
```

```python
import functools

import jax
import jax.numpy as jnp
import numpy as np
from jax import lax
from jax.experimental import pallas as pl
from jax.experimental.pallas import tpu as pltpu
from jax.sharding import PartitionSpec as P

NODES = 4
PASSES = 4

time_step = 0.25
diffusion = 4.0
reaction = 1.0

F32 = jnp.float32

OUTER = 5
SLAB = 8
HALF = 4


def collocation(count):
    points = [-0.8611363115940526, -0.3399810435848563, 0.3399810435848563, 0.8611363115940526]
    raw_weights = [0.3478548451374538, 0.6521451548625461, 0.6521451548625461, 0.3478548451374538]
    node_times = [(point + 1.0) / 2.0 for point in points]
    quadrature = [[0.0 for column in range(count)] for target in range(count)]
    for source in range(count):
        coeffs = [1.0]
        scaling = 1.0
        for other in range(count):
            if other != source:
                other_time = node_times[other]
                shifted = [0.0] + coeffs
                for power in range(len(coeffs)):
                    shifted[power] = shifted[power] - other_time * coeffs[power]
                coeffs = shifted
                scaling = scaling * (node_times[source] - other_time)
        for target in range(count):
            target_time = node_times[target]
            integral = 0.0
            for power in range(len(coeffs)):
                integral = integral + coeffs[power] * target_time ** (power + 1) / (power + 1)
            quadrature[target][source] = integral / scaling
    return (node_times, quadrature, [weight / 2.0 for weight in raw_weights])


LIN, CUB, WEIGHT, MIX, SCALE, FIRST, CORE, COUNT = 0, 16, 32, 36, 40, 44, 45, 46


def scalar_table():
    times, quad, weights = collocation(NODES)
    table = np.zeros((NODES, COUNT), np.float64)
    for node in range(NODES):
        order = [node, node ^ 2, node ^ 1, node ^ 3]
        for place, target in enumerate(order):
            implicit = time_step * diffusion * times[target]
            for index, source in enumerate(order):
                lin = time_step * diffusion * quad[target][source]
                table[node, LIN + 4 * place + index] = lin - (implicit if source == target else 0.0)
                table[node, CUB + 4 * place + index] = time_step * reaction * quad[target][source]
            table[node, WEIGHT + place] = weights[target]
            table[node, MIX + place] = implicit / (1.0 + 6.0 * implicit)
            table[node, SCALE + place] = 1.0 / (1.0 + 6.0 * implicit)
        table[node, CORE] = node & 1
    return table.astype(np.float32)


def flat_sum(plane):
    rows, columns = plane.shape
    vertical = pltpu.roll(plane, 1, 0) + pltpu.roll(plane, rows - 1, 0)
    return vertical + (pltpu.roll(plane, 1, 1) + pltpu.roll(plane, columns - 1, 1))


def around(outside, centre, inside):
    return (outside + inside) + flat_sum(centre)


def laplacian(outside, centre, inside):
    return around(outside, centre, inside) - 6.0 * centre


def mixed(scalars, base, planes):
    own, across, beside, corner = (scalars[base + index] * plane for index, plane in enumerate(planes))
    return (own + across) + (beside + corner)


def cubed(state):
    return state - state * state * state


def counter(scalars):
    upper = (scalars[CORE] > 0.5).astype(jnp.int32)
    base, sign = upper * (SLAB - 1), 1 - 2 * upper
    return lambda place: base + sign * (place - OUTER)


def send_kernel(scalars, own, beside, start, halo_a, halo_b, halo_start):
    plane = counter(scalars)
    for index in range(3):
        halo_a[index] = own[plane(10 + index)]
        halo_a[index + 3] = beside[plane(10 + index)]
    for index in range(2):
        halo_b[index] = own[plane(8 + index)]
        halo_b[index + 2] = beside[plane(8 + index)]
    for index in range(4):
        halo_start[index] = start[plane(9 + index)]


def end_kernel(scalars, own, across, beside, corner, start, near, away, total):
    plane = counter(scalars)
    total[0] = jnp.zeros_like(total[0])
    total[SLAB + 1] = jnp.zeros_like(total[0])
    sources = (own, across, beside, corner)
    for index in range(SLAB):
        total[index + 1] = mixed(scalars, WEIGHT, [source[plane(index + OUTER)] for source in sources])

    for index in range(SLAB):
        here = plane(index + OUTER)
        local = mixed(scalars, WEIGHT, [cubed(source[here]) for source in sources])
        force = diffusion * laplacian(total[index], total[index + 1], total[index + 2]) + reaction * local
        value = start[here] + time_step * force
        if index < HALF:
            near[index + 1] = value
        else:
            away[index - HALF] = value
    near[0] = (time_step * diffusion) * total[1]
    away[HALF] = (time_step * diffusion) * total[SLAB]


class Stack:
    def __init__(self, ref, places):
        self.ref, self.index = ref, {place: index for index, place in enumerate(places)}

    def __getitem__(self, key):
        target, place = key
        return self.ref[target, self.index[place]]

    def __setitem__(self, key, value):
        target, place = key
        self.ref[target, self.index[place]] = value

    def __contains__(self, place):
        return place in self.index


class Chain:
    def __init__(self, *stacks):
        self.stacks = stacks

    def find(self, place):
        return next(stack for stack in self.stacks if place in stack)

    def __getitem__(self, key):
        return self.find(key[1])[key]

    def __setitem__(self, key, value):
        self.find(key[1])[key] = value


STAGES = [
    {"v": range(5, 13), "r": range(5, 12), "g": range(6, 12), "x1": range(6, 12), "x2": range(7, 11), "x3": range(8, 10), "x4": range(0)},
    {"v": range(2, 5), "r": range(2, 5), "g": range(3, 6), "x1": range(3, 6), "x2": range(4, 7), "x3": range(5, 8), "x4": range(6, 9)},
    {"v": range(0, 2), "r": range(1, 2), "g": range(1, 3), "x1": range(1, 3), "x2": range(2, 4), "x3": range(3, 5), "x4": range(4, 6)},
]
NAMES = ("v", "r", "g", "x1", "x2", "x3", "x4")
KEPT = [
    {"v": (5, 6), "r": (5,), "g": (6, 7, 8), "x1": (6, 7), "x2": (7, 8), "x3": (8, 9), "x4": ()},
    {"v": (2, 3), "r": (2,), "g": (3, 4, 5), "x1": (3, 4), "x2": (4, 5), "x3": (5, 6), "x4": (6, 7, 8)},
]


def kept_count(stage):
    return sum(len(places) for places in KEPT[stage].values())


def kept_stacks(ref, stage):
    stacks, first = {}, 0
    for name in NAMES:
        places = KEPT[stage][name]
        stacks[name] = Stack(ref.at[:, first : first + len(places)], places) if places else Stack(None, ())
        first += len(places)
    return stacks


def run_stage(stage, scalars, state, old, new):
    both = {name: Chain(new[name], *(stacks[name] for stacks in old)) for name in NAMES}
    targets = range(NODES)
    for place in STAGES[stage]["v"]:
        states = [state(source, place) for source in range(NODES)]
        for target in targets:
            new["v"][target, place] = mixed(scalars, LIN + 4 * target, states)
        if place in STAGES[stage]["r"]:
            local = [cubed(value) for value in states]
            for target in targets:
                new["r"][target, place] = mixed(scalars, CUB + 4 * target, local)
    for place in STAGES[stage]["g"]:
        for target in targets:
            value = laplacian(*(both["v"][target, place + by] for by in (-1, 0, 1)))
            new["g"][target, place] = scalars[SCALE + target] * (value + both["r"][target, place])
    for name, before in (("x1", None), ("x2", "x1"), ("x3", "x2"), ("x4", "x3")):
        for place in STAGES[stage][name]:
            for target in targets:
                if before is None:
                    planes = [state(target, place + by) for by in (-1, 0, 1)]
                else:
                    planes = [both[before][target, place + by] for by in (-1, 0, 1)]
                new[name][target, place] = both["g"][target, place] + scalars[MIX + target] * around(*planes)


def stage_scratch(stage, planes):
    return [planes(NODES, len(STAGES[stage][name])) for name in NAMES if len(STAGES[stage][name])]


def stage_stacks(stage, refs):
    refs = iter(refs)
    return {name: Stack(next(refs), places) if len(places) else Stack(None, ()) for name, places in STAGES[stage].items()}


def keep(stage, new, out):
    kept = kept_stacks(out, stage)
    for name in NAMES:
        for place in KEPT[stage][name]:
            for target in range(NODES):
                kept[name][target, place] = new[name][target, place]


def first_kernel(scalars, own, across, beside, corner, out, *scratch):
    plane = counter(scalars)
    sources = (own, across, beside, corner)
    new = stage_stacks(0, scratch)
    run_stage(0, scalars, lambda source, place: sources[source][plane(place)], [], new)
    keep(0, new, out)


def halo_state(halo, halo_across, first, count):
    def state(source, place):
        ref = (halo, halo_across, halo, halo_across)[source]
        return ref[(count if source >= 2 else 0) + place - first]

    return state


def second_kernel(scalars, own, across, beside, corner, halo_a, across_a, kept, out, *scratch):
    plane = counter(scalars)
    sources = (own, across, beside, corner)
    outer = halo_state(halo_a, across_a, 2, 3)

    def state(source, place):
        return outer(source, place) if place < OUTER else sources[source][plane(place)]

    new = stage_stacks(1, scratch)
    run_stage(1, scalars, state, [kept_stacks(kept, 0)], new)
    keep(1, new, out)


def third_kernel(scalars, halo_a, across_a, halo_b, across_b, kept, out, *scratch):
    inner, outer = halo_state(halo_a, across_a, 2, 3), halo_state(halo_b, across_b, 0, 2)

    def state(source, place):
        return outer(source, place) if place < 2 else inner(source, place)

    new = stage_stacks(2, scratch)
    old = kept_stacks(kept, 1)
    run_stage(2, scalars, state, [old], new)
    for target in range(NODES):
        for place in range(4, 9):
            source = new if place in new["x4"] else old
            out[target, place - 4] = source["x4"][target, place]


def last_kernel(scalars, start, halo_start, near, far, away, part, mine, swap, begin, once, twice, last, total):
    plane = counter(scalars)
    first = scalars[FIRST]
    for place in range(1, 4):
        begin[place] = halo_start[place - 1] + away[place - 1]
    begin[4] = (halo_start[3] + away[3]) + near[0]
    begin[5] = (first * start[plane(5)] + near[1]) + away[4]
    for place in range(6, 9):
        begin[place] = first * start[plane(place)] + near[place - 4]
    for place in range(9, 12):
        begin[place] = first * start[plane(place)] + far[11 - place]

    for place in range(2, 11):
        once[place] = around(*(begin[place + by] for by in (-1, 0, 1)))
    for place in range(3, 10):
        twice[place] = around(*(once[place + by] for by in (-1, 0, 1)))
    for place in range(4, 9):
        thrice = around(*(twice[place + by] for by in (-1, 0, 1)))
        for target in range(NODES):
            mix = scalars[MIX + target]
            value = begin[place] + mix * (once[place] + mix * (twice[place] + mix * thrice))
            last[target, place - 4] = part[target, place - 4] + scalars[SCALE + target] * value
        total[place - 4] = mixed(scalars, WEIGHT, [last[target, place - 4] for target in range(NODES)])
    total[5] = jnp.zeros_like(total[5])
    for place in range(OUTER, OUTER + HALF):
        index = place - 4
        local = mixed(scalars, WEIGHT, [cubed(last[target, index]) for target in range(NODES)])
        force = diffusion * laplacian(total[index - 1], total[index], total[index + 1]) + reaction * local
        mine[index - 1] = last[0, index]
        mine[index - 1 + HALF] = begin[place] + time_step * force
        swap[index - 1] = last[2, index]
        swap[index - 1 + HALF] = begin[place] + time_step * force
    mine[2 * HALF] = total[HALF]
    swap[2 * HALF] = total[HALF]


def join_kernel(scalars, mine, other, state, end):
    plane = counter(scalars)
    for index in range(HALF):
        near, far = plane(OUTER + index), plane(OUTER + SLAB - 1 - index)
        state[near] = mine[index]
        state[far] = other[index]
        own, others = mine[HALF + index], other[HALF + index]
        if index == HALF - 1:
            own = own + (time_step * diffusion) * other[2 * HALF]
            others = others + (time_step * diffusion) * mine[2 * HALF]
        end[near] = own
        end[far] = others


def call(kernel, scalars, operands, outs, scratch, limit):
    return pl.pallas_call(
        kernel,
        out_shape=[jax.ShapeDtypeStruct(shape, F32) for shape in outs],
        in_specs=[pl.BlockSpec(memory_space=pltpu.SMEM)] + [pl.BlockSpec(memory_space=pltpu.VMEM)] * len(operands),
        out_specs=[pl.BlockSpec(memory_space=pltpu.VMEM)] * len(outs),
        scratch_shapes=[pltpu.VMEM(shape, F32) for shape in scratch],
        compiler_params=pltpu.CompilerParams(vmem_limit_bytes=limit << 20),
        cost_estimate=pl.CostEstimate(flops=1000, bytes_accessed=1000, transcendentals=0),
    )(scalars, *operands)


def on_device(start_old, nodes_old):
    slabs, slices = lax.axis_size("space"), lax.axis_size("tm")
    node_index = lax.axis_index("node")
    slice_index = lax.axis_index("tm")
    state, start = nodes_old[0, 0], start_old[0]
    slab, rows, columns = state.shape
    scalars = jnp.asarray(scalar_table())[node_index]
    scalars = scalars.at[FIRST].set((slice_index == 0).astype(F32))

    def after(array, other):
        return lax.optimization_barrier((array, other))[0]

    def planes(*lead):
        return (*lead, rows, columns)

    def across(array):
        return lax.ppermute(array, "node", [(node, node ^ 2) for node in range(NODES)])

    def beside(array):
        return lax.ppermute(array, "node", [(node, node ^ 1) for node in range(NODES)])

    always = scalars[WEIGHT] > 0.0

    def swapped(array):
        return lax.cond(always, beside, lambda array: array, array)

    def device(slab_, node, slice_):
        return ((slab_ % slabs) * NODES + node) * slices + slice_

    def spread(array, steps, by):
        pairs = [
            (device(slab_, node, here), device(slab_ + by[node % 2], node, there))
            for slab_ in range(slabs) for node in range(NODES) for here, there in steps
        ]
        return lax.ppermute(array, ("space", "node", "tm"), pairs)

    same = [(slice_, slice_) for slice_ in range(slices)]
    onward = [(slice_, slice_ + 1) for slice_ in range(slices - 1)]

    beside_state = beside(state)
    across_state = across(state)
    send_a, send_b, send_start = call(
        send_kernel, scalars, [state, beside_state, start], [planes(6), planes(4), planes(4)], [], 16
    )
    halo_a = spread(send_a, same, (1, -1))
    halo_b = spread(send_b, same, (1, -1))
    corner_state = swapped(after(across_state, send_a))
    sources = [state, across_state, beside_state, corner_state]
    send_near, send_away = call(end_kernel, scalars, [*sources, start], [planes(5)] * 2, [planes(slab + 2)], 16)
    near = spread(send_near, onward, (0, 0))
    away = spread(send_away, onward, (1, -1))
    across_a = across(after(halo_a, across_state))
    across_b = across(halo_b)
    halo_start = spread(after(send_start, corner_state), [(0, 0)], (1, -1))

    (kept,) = call(first_kernel, scalars, sources, [planes(NODES, kept_count(0))], stage_scratch(0, planes), 30)
    (kept,) = call(
        second_kernel, scalars, [*sources, halo_a, across_a, kept], [planes(NODES, kept_count(1))], stage_scratch(1, planes), 24
    )
    (part,) = call(
        third_kernel, scalars, [halo_a, across_a, halo_b, across_b, kept], [planes(NODES, 5)], stage_scratch(2, planes), 24
    )
    far = beside(after(near, part)[2:])
    mine, swap = call(
        last_kernel, scalars, [start, halo_start, near, far, away, part], [planes(2 * HALF + 1)] * 2,
        [planes(12), planes(11), planes(10), planes(NODES, 5), planes(6)], 24,
    )
    state_new, end_new = call(join_kernel, scalars, [mine, beside(swap)], [planes(slab)] * 2, [], 16)
    return (state_new[None, None], end_new[None])


def solution(mesh):
    return jax.shard_map(
        on_device,
        mesh=mesh,
        in_specs=(P("tm", "space", None, None), P("tm", "node", "space", None, None)),
        out_specs=(P("tm", "node", "space", None, None), P("tm", "space", None, None)),
        check_vma=False,
    )
```

```python
import functools

import jax
import jax.numpy as jnp
import numpy as np
from jax import lax
from jax.experimental import pallas as pl
from jax.experimental.pallas import tpu as pltpu
from jax.sharding import PartitionSpec as P

NODES = 4
PASSES = 4

time_step = 0.25
diffusion = 4.0
reaction = 1.0

F32 = jnp.float32

OUTER = 5
SLAB = 8
HALF = 4


def collocation(count):
    points = [-0.8611363115940526, -0.3399810435848563, 0.3399810435848563, 0.8611363115940526]
    raw_weights = [0.3478548451374538, 0.6521451548625461, 0.6521451548625461, 0.3478548451374538]
    node_times = [(point + 1.0) / 2.0 for point in points]
    quadrature = [[0.0 for column in range(count)] for target in range(count)]
    for source in range(count):
        coeffs = [1.0]
        scaling = 1.0
        for other in range(count):
            if other != source:
                other_time = node_times[other]
                shifted = [0.0] + coeffs
                for power in range(len(coeffs)):
                    shifted[power] = shifted[power] - other_time * coeffs[power]
                coeffs = shifted
                scaling = scaling * (node_times[source] - other_time)
        for target in range(count):
            target_time = node_times[target]
            integral = 0.0
            for power in range(len(coeffs)):
                integral = integral + coeffs[power] * target_time ** (power + 1) / (power + 1)
            quadrature[target][source] = integral / scaling
    return (node_times, quadrature, [weight / 2.0 for weight in raw_weights])


LIN, CUB, WEIGHT, MIX, SCALE, FIRST, CORE, COUNT = 0, 16, 32, 36, 40, 44, 45, 46


def scalar_table():
    times, quad, weights = collocation(NODES)
    table = np.zeros((NODES, COUNT), np.float64)
    for node in range(NODES):
        order = [node, node ^ 2, node ^ 1, node ^ 3]
        for place, target in enumerate(order):
            implicit = time_step * diffusion * times[target]
            scale = 1.0 / (1.0 + 6.0 * implicit)
            for index, source in enumerate(order):
                lin = time_step * diffusion * quad[target][source] - (implicit if source == target else 0.0)
                table[node, LIN + 4 * place + index] = scale * lin
                table[node, CUB + 4 * place + index] = scale * time_step * reaction * quad[target][source]
            table[node, WEIGHT + place] = weights[target]
            table[node, MIX + place] = scale * implicit
            table[node, SCALE + place] = scale
        table[node, CORE] = node & 1
    return table.astype(np.float32)


class Plane:
    def __init__(self, ref, *index):
        self.ref, self.index = ref, index

    def rows(self, first, count):
        return self.ref[(*self.index, pl.ds(first, count))]

    def put(self, first, value):
        self.ref[(*self.index, pl.ds(first, value.shape[0]))] = value


def flat_sum(plane, first, count):
    whole = plane.ref.shape[-2]
    centre = plane.rows(first, count)
    above, below = plane.rows((first - 8) % whole, 8), plane.rows((first + count) % whole, 8)
    longer = jnp.concatenate([above, centre, below], axis=0)
    vertical = pltpu.roll(longer, 1, 0)[8 : 8 + count] + pltpu.roll(longer, count + 15, 0)[8 : 8 + count]
    columns = centre.shape[1]
    return vertical + (pltpu.roll(centre, 1, 1) + pltpu.roll(centre, columns - 1, 1)), centre


def around(outside, plane, inside, first, count):
    flat, centre = flat_sum(plane, first, count)
    return (outside.rows(first, count) + inside.rows(first, count)) + flat, centre


def chunks(plane, count):
    return range(0, plane.ref.shape[-2], count)


def mixed(scalars, base, planes):
    own, across, beside, corner = (scalars[base + index] * plane for index, plane in enumerate(planes))
    return (own + across) + (beside + corner)


def cubed(state):
    return state - state * state * state


def counter(scalars):
    upper = (scalars[CORE] > 0.5).astype(jnp.int32)
    base, sign = upper * (SLAB - 1), 1 - 2 * upper
    return lambda place: base + sign * (place - OUTER)


def send_kernel(scalars, own, beside, halo_a, halo_b):
    plane = counter(scalars)
    for number, source in enumerate((own, beside)):
        for index in range(3):
            halo_a[index + 3 * number] = source[plane(10 + index)]
        for index in range(2):
            halo_b[index + 2 * number] = source[plane(8 + index)]


def end_kernel(scalars, own, across, beside, corner, start, near, away, total):
    plane = counter(scalars)
    sources = (own, across, beside, corner)
    weighted = [Plane(total, index) for index in range(SLAB + 2)]
    for first in chunks(weighted[0], 32):
        nothing = jnp.zeros_like(weighted[0].rows(first, 32))
        weighted[0].put(first, nothing)
        weighted[SLAB + 1].put(first, nothing)
        for index in range(SLAB):
            here = plane(index + OUTER)
            weighted[index + 1].put(first, mixed(scalars, WEIGHT, [Plane(source, here).rows(first, 32) for source in sources]))
    for index in range(SLAB):
        here = plane(index + OUTER)
        out = Plane(near, index + 1) if index < HALF else Plane(away, index - HALF)
        for first in chunks(out, 32):
            local = mixed(scalars, WEIGHT, [cubed(Plane(source, here).rows(first, 32)) for source in sources])
            nearby, centre = around(*weighted[index : index + 3], first, 32)
            force = diffusion * (nearby - 6.0 * centre) + reaction * local
            out.put(first, Plane(start, here).rows(first, 32) + time_step * force)
    near[0] = (time_step * diffusion) * total[1]
    away[HALF] = (time_step * diffusion) * total[SLAB]


NAMES = ("g", "x1", "x2", "x3", "x4")
STAGES = [
    {"g": range(6, 12), "x1": range(6, 12), "x2": range(7, 11), "x3": range(8, 10), "x4": ()},
    {"g": range(3, 6), "x1": range(3, 6), "x2": range(4, 7), "x3": range(5, 8), "x4": range(6, 9)},
    {"g": range(1, 3), "x1": range(1, 3), "x2": range(2, 4), "x3": range(3, 5), "x4": range(4, 6)},
]
KEPT = [
    {"g": (6, 7, 8), "x1": (6, 7), "x2": (7, 8), "x3": (8, 9), "x4": ()},
    {"g": (3, 4, 5), "x1": (3, 4), "x2": (4, 5), "x3": (5, 6), "x4": (6, 7, 8)},
    {"g": (), "x1": (), "x2": (), "x3": (), "x4": (4, 5)},
]


def kept_keys(stage):
    return [(name, place) for name in NAMES for place in KEPT[stage][name]]


def spare_keys(stage):
    return [(name, place) for name in NAMES for place in STAGES[stage][name] if place not in KEPT[stage][name]]


def run_stage(stage, scalars, state, old, out, spare):
    where = {}
    for ref, keys in ((old, kept_keys(stage - 1) if stage else []), (out, kept_keys(stage)), (spare, spare_keys(stage))):
        where.update({key: (ref, index) for index, key in enumerate(keys)})

    def plane(name, target, place):
        ref, index = where[name, place]
        return Plane(ref, target, index)

    targets = range(NODES)
    for place in STAGES[stage]["g"]:
        sources = [[state(source, place + by) for by in (-1, 0, 1)] for source in range(NODES)]
        for first in chunks(sources[0][0], 16):
            nearby, centre = zip(*(around(*planes, first, 16) for planes in sources))
            spread_ = [value - 6.0 * middle for value, middle in zip(nearby, centre)]
            local = [cubed(middle) for middle in centre]
            for target in targets:
                value = mixed(scalars, LIN + 4 * target, spread_) + mixed(scalars, CUB + 4 * target, local)
                plane("g", target, place).put(first, value)
                plane("x1", target, place).put(first, value + scalars[MIX + target] * nearby[target])
    for name, before in (("x2", "x1"), ("x3", "x2"), ("x4", "x3")):
        for place in STAGES[stage][name]:
            for target in targets:
                planes = [plane(before, target, place + by) for by in (-1, 0, 1)]
                base, sink = plane("g", target, place), plane(name, target, place)
                for first in chunks(sink, 32):
                    nearby, _ = around(*planes, first, 32)
                    sink.put(first, base.rows(first, 32) + scalars[MIX + target] * nearby)


def first_kernel(scalars, own, across, beside, corner, out, spare):
    plane = counter(scalars)
    sources = (own, across, beside, corner)
    run_stage(0, scalars, lambda source, place: Plane(sources[source], plane(place)), None, out, spare)


def halo_state(halo, halo_across, first, count):
    def state(source, place):
        ref = (halo, halo_across, halo, halo_across)[source]
        return Plane(ref, (count if source >= 2 else 0) + place - first)

    return state


def second_kernel(scalars, own, across, beside, corner, halo_a, across_a, kept, out, spare):
    plane = counter(scalars)
    sources = (own, across, beside, corner)
    outer = halo_state(halo_a, across_a, 2, 3)

    def state(source, place):
        return outer(source, place) if place < OUTER else Plane(sources[source], plane(place))

    run_stage(1, scalars, state, kept, out, spare)


def third_kernel(scalars, halo_a, across_a, halo_b, across_b, kept, out, spare):
    inner, outer = halo_state(halo_a, across_a, 2, 3), halo_state(halo_b, across_b, 0, 2)

    def state(source, place):
        return outer(source, place) if place < 2 else inner(source, place)

    run_stage(2, scalars, state, kept, out, spare)


def last_kernel(scalars, start, halo_start, near, far, away, kept, part, mine, swap, begin, once, twice, last, total):
    plane = counter(scalars)
    begin_first = scalars[FIRST]
    back = (scalars[CORE] > 0.5).astype(jnp.int32)
    for place in range(1, 5):
        begin[place] = halo_start[place - 1 + back * (5 - 2 * place)] + away[place - 1]
    begin[4] = begin[4] + near[0]
    begin[5] = (begin_first * start[plane(5)] + near[1]) + away[4]
    for place in range(6, 9):
        begin[place] = begin_first * start[plane(place)] + near[place - 4]
    for place in range(9, 12):
        begin[place] = begin_first * start[plane(place)] + far[11 - place]

    def around_place(ref, place, first, count):
        return around(*(Plane(ref, place + by) for by in (-1, 0, 1)), first, count)

    for source, sink, places in ((begin, once, range(2, 11)), (once, twice, range(3, 10))):
        for place in places:
            out = Plane(sink, place)
            for first in chunks(out, 32):
                out.put(first, around_place(source, place, first, 32)[0])
    kept_x4 = {key: index for index, key in enumerate(kept_keys(1))}
    for place in range(4, 9):
        for first in chunks(Plane(total, 0), 16):
            thrice, two = around_place(twice, place, first, 16)
            zero, one = Plane(begin, place).rows(first, 16), Plane(once, place).rows(first, 16)
            values = []
            for target in range(NODES):
                mix = scalars[MIX + target]
                rest = Plane(part, target, place - 4) if place < 6 else Plane(kept, target, kept_x4["x4", place])
                value = scalars[SCALE + target] * (zero + mix * (one + mix * (two + mix * thrice)))
                values.append(rest.rows(first, 16) + value)
                Plane(last, target, place - 4).put(first, values[-1])
            Plane(total, place - 4).put(first, mixed(scalars, WEIGHT, values))
    total[5] = jnp.zeros_like(total[5])
    for place in range(OUTER, OUTER + HALF):
        index = place - 4
        for first in chunks(Plane(total, 0), 16):
            states = [Plane(last, target, index).rows(first, 16) for target in range(NODES)]
            local = mixed(scalars, WEIGHT, [cubed(state) for state in states])
            nearby, centre = around_place(total, index, first, 16)
            force = diffusion * (nearby - 6.0 * centre) + reaction * local
            value = Plane(begin, place).rows(first, 16) + time_step * force
            for sink, state in ((mine, states[0]), (swap, states[2])):
                Plane(sink, index - 1).put(first, state)
                Plane(sink, index - 1 + HALF).put(first, value)
    mine[2 * HALF] = total[HALF]
    swap[2 * HALF] = total[HALF]


def join_kernel(scalars, mine, other, state, end):
    plane = counter(scalars)
    for index in range(HALF):
        near, far = plane(OUTER + index), plane(OUTER + SLAB - 1 - index)
        state[near] = mine[index]
        state[far] = other[index]
        own, others = mine[HALF + index], other[HALF + index]
        if index == HALF - 1:
            own = own + (time_step * diffusion) * other[2 * HALF]
            others = others + (time_step * diffusion) * mine[2 * HALF]
        end[near] = own
        end[far] = others


def call(kernel, scalars, operands, outs, scratch, limit):
    return pl.pallas_call(
        kernel,
        out_shape=[jax.ShapeDtypeStruct(shape, F32) for shape in outs],
        in_specs=[pl.BlockSpec(memory_space=pltpu.SMEM)] + [pl.BlockSpec(memory_space=pltpu.VMEM)] * len(operands),
        out_specs=[pl.BlockSpec(memory_space=pltpu.VMEM)] * len(outs),
        scratch_shapes=[pltpu.VMEM(shape, F32) for shape in scratch],
        compiler_params=pltpu.CompilerParams(vmem_limit_bytes=limit << 20),
        cost_estimate=pl.CostEstimate(flops=1000, bytes_accessed=1000, transcendentals=0),
    )(scalars, *operands)


def on_device(start_old, nodes_old):
    slabs, slices = lax.axis_size("space"), lax.axis_size("tm")
    node_index = lax.axis_index("node")
    slice_index = lax.axis_index("tm")
    state, start = nodes_old[0, 0], start_old[0]
    slab, rows, columns = state.shape
    scalars = jnp.asarray(scalar_table())[node_index]
    scalars = scalars.at[FIRST].set((slice_index == 0).astype(F32))

    def after(array, other):
        return lax.optimization_barrier((array, other))[0]

    def planes(*lead):
        return (*lead, rows, columns)

    def across(array):
        return lax.ppermute(array, "node", [(node, node ^ 2) for node in range(NODES)])

    def beside(array):
        return lax.ppermute(array, "node", [(node, node ^ 1) for node in range(NODES)])

    always = scalars[WEIGHT] > 0.0

    def swapped(array):
        return lax.cond(always, beside, lambda array: array, array)

    def device(slab_, node, slice_):
        return ((slab_ % slabs) * NODES + node) * slices + slice_

    def spread(array, steps, by):
        pairs = [
            (device(slab_, node, here), device(slab_ + by[node % 2], node, there))
            for slab_ in range(slabs) for node in range(NODES) for here, there in steps
        ]
        return lax.ppermute(array, ("space", "node", "tm"), pairs)

    same = [(slice_, slice_) for slice_ in range(slices)]
    onward = [(slice_, slice_ + 1) for slice_ in range(slices - 1)]

    beside_state = beside(state)
    across_state = across(state)
    send_a, send_b = call(send_kernel, scalars, [state, beside_state], [planes(6), planes(4)], [], 16)
    halo_a = spread(send_a, same, (1, -1))
    halo_b = spread(send_b, same, (1, -1))
    corner_state = swapped(after(across_state, send_a))
    sources = [state, across_state, beside_state, corner_state]
    first_start = lax.dynamic_slice_in_dim(start, HALF * (1 - lax.rem(node_index, 2)), HALF, axis=0)
    passing_start = spread(first_start, [(0, 1)], (0, 0))
    send_near, send_away = call(
        end_kernel, scalars, [*sources, after(start, passing_start)], [planes(5), planes(5)], [planes(slab + 2)], 16
    )
    near = spread(send_near, onward, (0, 0))
    away = spread(send_away, onward, (1, -1))
    across_a = across(after(halo_a, corner_state))
    halo_start = spread(passing_start, [(1, 0)], (1, -1))

    def stage(index, kernel, operands, limit):
        shapes = [planes(NODES, len(keys)) for keys in (kept_keys(index), spare_keys(index))]
        return call(kernel, scalars, operands, shapes[:1], shapes[1:], limit)[0]

    kept = stage(0, first_kernel, sources, 24)
    across_b = across(halo_b)
    kept = stage(1, second_kernel, [*sources, halo_a, across_a, kept], 24)
    part = stage(2, third_kernel, [halo_a, across_a, halo_b, across_b, kept], 24)
    far = beside(after(near, part)[2:])
    mine, swap = call(
        last_kernel, scalars, [start, halo_start, near, far, away, kept, part], [planes(2 * HALF + 1)] * 2,
        [planes(12), planes(11), planes(10), planes(NODES, 5), planes(6)], 24,
    )
    state_new, end_new = call(join_kernel, scalars, [mine, beside(swap)], [planes(slab)] * 2, [], 16)
    return (state_new[None, None], end_new[None])


def solution(mesh):
    return jax.shard_map(
        on_device,
        mesh=mesh,
        in_specs=(P("tm", "space", None, None), P("tm", "node", "space", None, None)),
        out_specs=(P("tm", "node", "space", None, None), P("tm", "space", None, None)),
        check_vma=False,
    )
```

```python
import functools

import jax
import jax.numpy as jnp
import numpy as np
from jax import lax
from jax.experimental import pallas as pl
from jax.experimental.pallas import tpu as pltpu
from jax.sharding import PartitionSpec as P

NODES = 4
PASSES = 4

time_step = 0.25
diffusion = 4.0
reaction = 1.0

F32 = jnp.float32

OUTER = 5
SLAB = 8
HALF = 4
RIGHT_ROWS, PASS_ROWS = 16, 32


def collocation(count):
    points = [-0.8611363115940526, -0.3399810435848563, 0.3399810435848563, 0.8611363115940526]
    raw_weights = [0.3478548451374538, 0.6521451548625461, 0.6521451548625461, 0.3478548451374538]
    node_times = [(point + 1.0) / 2.0 for point in points]
    quadrature = [[0.0 for column in range(count)] for target in range(count)]
    for source in range(count):
        coeffs = [1.0]
        scaling = 1.0
        for other in range(count):
            if other != source:
                other_time = node_times[other]
                shifted = [0.0] + coeffs
                for power in range(len(coeffs)):
                    shifted[power] = shifted[power] - other_time * coeffs[power]
                coeffs = shifted
                scaling = scaling * (node_times[source] - other_time)
        for target in range(count):
            target_time = node_times[target]
            integral = 0.0
            for power in range(len(coeffs)):
                integral = integral + coeffs[power] * target_time ** (power + 1) / (power + 1)
            quadrature[target][source] = integral / scaling
    return (node_times, quadrature, [weight / 2.0 for weight in raw_weights])


LIN, CUB, WEIGHT, MIX, SCALE, FIRST, CORE, COUNT = 0, 16, 32, 36, 40, 44, 45, 46


def scalar_table():
    times, quad, weights = collocation(NODES)
    table = np.zeros((NODES, COUNT), np.float64)
    for node in range(NODES):
        order = [node, node ^ 2, node ^ 1, node ^ 3]
        for place, target in enumerate(order):
            implicit = time_step * diffusion * times[target]
            scale = 1.0 / (1.0 + 6.0 * implicit)
            for index, source in enumerate(order):
                lin = time_step * diffusion * quad[target][source] - (implicit if source == target else 0.0)
                table[node, LIN + 4 * place + index] = scale * lin
                table[node, CUB + 4 * place + index] = scale * time_step * reaction * quad[target][source]
            table[node, WEIGHT + place] = weights[target]
            table[node, MIX + place] = scale * implicit
            table[node, SCALE + place] = scale
        table[node, CORE] = node & 1
    return table.astype(np.float32)


class Plane:
    def __init__(self, ref, *index):
        self.ref, self.index = ref, index

    def rows(self, first, count):
        return self.ref[(*self.index, pl.ds(first, count))]

    def put(self, first, value):
        self.ref[(*self.index, pl.ds(first, value.shape[0]))] = value


def flat_sum(plane, first, count):
    whole = plane.ref.shape[-2]
    centre = plane.rows(first, count)
    above, below = plane.rows((first - 8) % whole, 8), plane.rows((first + count) % whole, 8)
    longer = jnp.concatenate([above, centre, below], axis=0)
    vertical = pltpu.roll(longer, 1, 0)[8 : 8 + count] + pltpu.roll(longer, count + 15, 0)[8 : 8 + count]
    columns = centre.shape[1]
    return vertical + (pltpu.roll(centre, 1, 1) + pltpu.roll(centre, columns - 1, 1)), centre


def around(outside, plane, inside, first, count):
    flat, centre = flat_sum(plane, first, count)
    return (outside.rows(first, count) + inside.rows(first, count)) + flat, centre


def chunks(plane, count):
    return range(0, plane.ref.shape[-2], count)


def mixed(scalars, base, planes):
    own, across, beside, corner = (scalars[base + index] * plane for index, plane in enumerate(planes))
    return (own + across) + (beside + corner)


def cubed(state):
    return state - state * state * state


def counter(scalars):
    upper = (scalars[CORE] > 0.5).astype(jnp.int32)
    base, sign = upper * (SLAB - 1), 1 - 2 * upper
    return lambda place: base + sign * (place - OUTER)


def send_kernel(scalars, own, beside, halo_a, halo_b):
    plane = counter(scalars)
    for number, source in enumerate((own, beside)):
        for index in range(3):
            halo_a[index + 3 * number] = source[plane(10 + index)]
        for index in range(2):
            halo_b[index + 2 * number] = source[plane(8 + index)]


def end_kernel(scalars, own, across, beside, corner, start, out, total):
    plane = counter(scalars)
    sources = (own, across, beside, corner)
    weighted = [Plane(total, index) for index in range(HALF + 2)]

    def states(place, first):
        return [Plane(source, plane(place)).rows(first, 32) for source in sources]

    for first in chunks(weighted[0], 32):
        weighted[0].put(first, jnp.zeros_like(weighted[0].rows(first, 32)))
        for index in range(1, HALF + 2):
            value = mixed(scalars, WEIGHT, states(index + 4, first))
            weighted[index].put(first, value)
            if index == 1:
                Plane(out, 0).put(first, (time_step * diffusion) * value)
    for index in range(1, HALF + 1):
        place = index + 4
        for first in chunks(weighted[0], 32):
            local = mixed(scalars, WEIGHT, [cubed(state) for state in states(place, first)])
            nearby, centre = around(*weighted[index - 1 : index + 2], first, 32)
            force = diffusion * (nearby - 6.0 * centre) + reaction * local
            Plane(out, index).put(first, Plane(start, plane(place)).rows(first, 32) + time_step * force)


NAMES = ("g", "x1", "x2", "x3", "x4")
STAGES = [
    {"g": range(6, 12), "x1": range(6, 12), "x2": range(7, 11), "x3": range(8, 10), "x4": ()},
    {"g": range(3, 6), "x1": range(3, 6), "x2": range(4, 7), "x3": range(5, 8), "x4": range(6, 9)},
    {"g": range(1, 3), "x1": range(1, 3), "x2": range(2, 4), "x3": range(3, 5), "x4": range(4, 6)},
]
KEPT = [
    {"g": (6, 7, 8), "x1": (6, 7), "x2": (7, 8), "x3": (8, 9), "x4": ()},
    {"g": (3, 4, 5), "x1": (3, 4), "x2": (4, 5), "x3": (5, 6), "x4": (6, 7, 8)},
    {"g": (), "x1": (), "x2": (), "x3": (), "x4": (4, 5)},
]


def kept_keys(stage):
    return [(name, place) for name in NAMES for place in KEPT[stage][name]]


def spare_keys(stage):
    return [(name, place) for name in NAMES for place in STAGES[stage][name] if place not in KEPT[stage][name]]


def run_stage(stage, scalars, state, old, out, spare):
    where = {}
    for ref, keys in ((old, kept_keys(stage - 1) if stage else []), (out, kept_keys(stage)), (spare, spare_keys(stage))):
        where.update({key: (ref, index) for index, key in enumerate(keys)})

    def plane(name, target, place):
        ref, index = where[name, place]
        return Plane(ref, target, index)

    targets = range(NODES)
    for place in STAGES[stage]["g"]:
        sources = [[state(source, place + by) for by in (-1, 0, 1)] for source in range(NODES)]
        for first in chunks(sources[0][0], RIGHT_ROWS):
            nearby, centre = zip(*(around(*planes, first, RIGHT_ROWS) for planes in sources))
            spread_ = [value - 6.0 * middle for value, middle in zip(nearby, centre)]
            local = [cubed(middle) for middle in centre]
            for target in targets:
                value = mixed(scalars, LIN + 4 * target, spread_) + mixed(scalars, CUB + 4 * target, local)
                plane("g", target, place).put(first, value)
                plane("x1", target, place).put(first, value + scalars[MIX + target] * nearby[target])
    for name, before in (("x2", "x1"), ("x3", "x2"), ("x4", "x3")):
        for place in STAGES[stage][name]:
            for target in targets:
                planes = [plane(before, target, place + by) for by in (-1, 0, 1)]
                base, sink = plane("g", target, place), plane(name, target, place)
                for first in chunks(sink, PASS_ROWS):
                    nearby, _ = around(*planes, first, PASS_ROWS)
                    sink.put(first, base.rows(first, PASS_ROWS) + scalars[MIX + target] * nearby)


def first_kernel(scalars, own, across, beside, corner, out, spare):
    plane = counter(scalars)
    sources = (own, across, beside, corner)
    run_stage(0, scalars, lambda source, place: Plane(sources[source], plane(place)), None, out, spare)


def halo_state(halo, halo_across, first, count):
    def state(source, place):
        ref = (halo, halo_across, halo, halo_across)[source]
        return Plane(ref, (count if source >= 2 else 0) + place - first)

    return state


def second_kernel(scalars, own, across, beside, corner, halo_a, across_a, kept, out, spare):
    plane = counter(scalars)
    sources = (own, across, beside, corner)
    outer = halo_state(halo_a, across_a, 2, 3)

    def state(source, place):
        return outer(source, place) if place < OUTER else Plane(sources[source], plane(place))

    run_stage(1, scalars, state, kept, out, spare)


def third_kernel(scalars, halo_a, across_a, halo_b, across_b, kept, out, spare):
    inner, outer = halo_state(halo_a, across_a, 2, 3), halo_state(halo_b, across_b, 0, 2)

    def state(source, place):
        return outer(source, place) if place < 2 else inner(source, place)

    run_stage(2, scalars, state, kept, out, spare)


def last_kernel(scalars, start, halo_start, near, far, away, kept, part, mine, swap, begin, once, twice, last, total):
    plane = counter(scalars)
    begin_first = scalars[FIRST]
    back = (scalars[CORE] > 0.5).astype(jnp.int32)
    for place in range(1, 5):
        begin[place] = halo_start[place - 1 + back * (5 - 2 * place)] + away[5 - place]
    begin[4] = begin[4] + near[0]
    begin[5] = (begin_first * start[plane(5)] + near[1]) + away[0]
    for place in range(6, 9):
        begin[place] = begin_first * start[plane(place)] + near[place - 4]
    for place in range(9, 12):
        begin[place] = begin_first * start[plane(place)] + far[11 - place]

    def around_place(ref, place, first, count):
        return around(*(Plane(ref, place + by) for by in (-1, 0, 1)), first, count)

    for source, sink, places in ((begin, once, range(2, 11)), (once, twice, range(3, 10))):
        for place in places:
            out = Plane(sink, place)
            for first in chunks(out, 32):
                out.put(first, around_place(source, place, first, 32)[0])
    kept_x4 = {key: index for index, key in enumerate(kept_keys(1))}
    for place in range(4, 9):
        for first in chunks(Plane(total, 0), 16):
            thrice, two = around_place(twice, place, first, 16)
            zero, one = Plane(begin, place).rows(first, 16), Plane(once, place).rows(first, 16)
            values = []
            for target in range(NODES):
                mix = scalars[MIX + target]
                rest = Plane(part, target, place - 4) if place < 6 else Plane(kept, target, kept_x4["x4", place])
                value = scalars[SCALE + target] * (zero + mix * (one + mix * (two + mix * thrice)))
                values.append(rest.rows(first, 16) + value)
                Plane(last, target, place - 4).put(first, values[-1])
            Plane(total, place - 4).put(first, mixed(scalars, WEIGHT, values))
    total[5] = jnp.zeros_like(total[5])
    for place in range(OUTER, OUTER + HALF):
        index = place - 4
        for first in chunks(Plane(total, 0), 16):
            states = [Plane(last, target, index).rows(first, 16) for target in range(NODES)]
            local = mixed(scalars, WEIGHT, [cubed(state) for state in states])
            nearby, centre = around_place(total, index, first, 16)
            force = diffusion * (nearby - 6.0 * centre) + reaction * local
            value = Plane(begin, place).rows(first, 16) + time_step * force
            for sink, state in ((mine, states[0]), (swap, states[2])):
                Plane(sink, index - 1).put(first, state)
                Plane(sink, index - 1 + HALF).put(first, value)
    mine[2 * HALF] = total[HALF]
    swap[2 * HALF] = total[HALF]


def join_kernel(scalars, mine, other, state, end):
    plane = counter(scalars)
    for index in range(HALF):
        near, far = plane(OUTER + index), plane(OUTER + SLAB - 1 - index)
        state[near] = mine[index]
        state[far] = other[index]
        own, others = mine[HALF + index], other[HALF + index]
        if index == HALF - 1:
            own = own + (time_step * diffusion) * other[2 * HALF]
            others = others + (time_step * diffusion) * mine[2 * HALF]
        end[near] = own
        end[far] = others


def call(kernel, scalars, operands, outs, scratch, limit):
    return pl.pallas_call(
        kernel,
        out_shape=[jax.ShapeDtypeStruct(shape, F32) for shape in outs],
        in_specs=[pl.BlockSpec(memory_space=pltpu.SMEM)] + [pl.BlockSpec(memory_space=pltpu.VMEM)] * len(operands),
        out_specs=[pl.BlockSpec(memory_space=pltpu.VMEM)] * len(outs),
        scratch_shapes=[pltpu.VMEM(shape, F32) for shape in scratch],
        compiler_params=pltpu.CompilerParams(vmem_limit_bytes=limit << 20),
        cost_estimate=pl.CostEstimate(flops=1000, bytes_accessed=1000, transcendentals=0),
    )(scalars, *operands)


def on_device(start_old, nodes_old):
    slabs, slices = lax.axis_size("space"), lax.axis_size("tm")
    node_index = lax.axis_index("node")
    slice_index = lax.axis_index("tm")
    state, start = nodes_old[0, 0], start_old[0]
    slab, rows, columns = state.shape
    scalars = jnp.asarray(scalar_table())[node_index]
    scalars = scalars.at[FIRST].set((slice_index == 0).astype(F32))

    def after(array, other):
        return lax.optimization_barrier((array, other))[0]

    def planes(*lead):
        return (*lead, rows, columns)

    def across(array):
        return lax.ppermute(array, "node", [(node, node ^ 2) for node in range(NODES)])

    def beside(array):
        return lax.ppermute(array, "node", [(node, node ^ 1) for node in range(NODES)])

    always = scalars[WEIGHT] > 0.0

    def swapped(array):
        return lax.cond(always, beside, lambda array: array, array)

    def device(slab_, node, slice_):
        return ((slab_ % slabs) * NODES + node) * slices + slice_

    def spread(array, steps, by, flip=0):
        pairs = [
            (device(slab_, node, here), device(slab_ + by[node % 2], node ^ flip, there))
            for slab_ in range(slabs) for node in range(NODES) for here, there in steps
        ]
        return lax.ppermute(array, ("space", "node", "tm"), pairs)

    same = [(slice_, slice_) for slice_ in range(slices)]
    onward = [(slice_, slice_ + 1) for slice_ in range(slices - 1)]

    beside_state = beside(state)
    across_state = across(state)
    send_a, send_b = call(send_kernel, scalars, [state, beside_state], [planes(6), planes(4)], [], 16)
    halo_a = spread(send_a, same, (1, -1))
    halo_b = spread(send_b, same, (1, -1))
    corner_state = swapped(after(across_state, send_a))
    sources = [state, across_state, beside_state, corner_state]
    first_start = lax.dynamic_slice_in_dim(start, HALF * (1 - lax.rem(node_index, 2)), HALF, axis=0)
    passing_start = spread(first_start, [(0, 1)], (0, 0))
    (send_end,) = call(
        end_kernel, scalars, [*sources, after(start, passing_start)], [planes(5)], [planes(HALF + 2)], 16
    )
    near = spread(send_end, onward, (0, 0))
    away = spread(send_end, onward, (-1, 1), 1)
    across_a = across(after(halo_a, corner_state))
    halo_start = spread(passing_start, [(1, 0)], (1, -1))

    def stage(index, kernel, operands, limit):
        shapes = [planes(NODES, len(keys)) for keys in (kept_keys(index), spare_keys(index))]
        return call(kernel, scalars, operands, shapes[:1], shapes[1:], limit)[0]

    kept = stage(0, first_kernel, sources, 24)
    across_b = across(after(halo_b, kept))
    kept = stage(1, second_kernel, [*sources, halo_a, across_a, kept], 24)
    part = stage(2, third_kernel, [halo_a, across_a, halo_b, across_b, kept], 24)
    far = beside(after(near, part)[2:])
    mine, swap = call(
        last_kernel, scalars, [start, halo_start, near, far, away, kept, part], [planes(2 * HALF + 1)] * 2,
        [planes(12), planes(11), planes(10), planes(NODES, 5), planes(6)], 24,
    )
    state_new, end_new = call(join_kernel, scalars, [mine, beside(swap)], [planes(slab)] * 2, [], 16)
    return (state_new[None, None], end_new[None])


def solution(mesh):
    return jax.shard_map(
        on_device,
        mesh=mesh,
        in_specs=(P("tm", "space", None, None), P("tm", "node", "space", None, None)),
        out_specs=(P("tm", "node", "space", None, None), P("tm", "space", None, None)),
        check_vma=False,
    )
```

```python
import functools

import jax
import jax.numpy as jnp
import numpy as np
from jax import lax
from jax.experimental import pallas as pl
from jax.experimental.pallas import tpu as pltpu
from jax.sharding import PartitionSpec as P

NODES = 4
PASSES = 4

time_step = 0.25
diffusion = 4.0
reaction = 1.0

F32 = jnp.float32

OUTER = 5
SLAB = 8
HALF = 4
RIGHT_ROWS, PASS_ROWS = 16, 32


def collocation(count):
    points = [-0.8611363115940526, -0.3399810435848563, 0.3399810435848563, 0.8611363115940526]
    raw_weights = [0.3478548451374538, 0.6521451548625461, 0.6521451548625461, 0.3478548451374538]
    node_times = [(point + 1.0) / 2.0 for point in points]
    quadrature = [[0.0 for column in range(count)] for target in range(count)]
    for source in range(count):
        coeffs = [1.0]
        scaling = 1.0
        for other in range(count):
            if other != source:
                other_time = node_times[other]
                shifted = [0.0] + coeffs
                for power in range(len(coeffs)):
                    shifted[power] = shifted[power] - other_time * coeffs[power]
                coeffs = shifted
                scaling = scaling * (node_times[source] - other_time)
        for target in range(count):
            target_time = node_times[target]
            integral = 0.0
            for power in range(len(coeffs)):
                integral = integral + coeffs[power] * target_time ** (power + 1) / (power + 1)
            quadrature[target][source] = integral / scaling
    return (node_times, quadrature, [weight / 2.0 for weight in raw_weights])


LIN, CUB, WEIGHT, MIX, SCALE, FIRST, CORE, COUNT = 0, 16, 32, 36, 40, 44, 45, 46


def scalar_table():
    times, quad, weights = collocation(NODES)
    table = np.zeros((NODES, COUNT), np.float64)
    for node in range(NODES):
        order = [node, node ^ 2, node ^ 1, node ^ 3]
        for place, target in enumerate(order):
            implicit = time_step * diffusion * times[target]
            scale = 1.0 / (1.0 + 6.0 * implicit)
            for index, source in enumerate(order):
                lin = time_step * diffusion * quad[target][source] - (implicit if source == target else 0.0)
                table[node, LIN + 4 * place + index] = scale * lin
                table[node, CUB + 4 * place + index] = scale * time_step * reaction * quad[target][source]
            table[node, WEIGHT + place] = weights[target]
            table[node, MIX + place] = scale * implicit
            table[node, SCALE + place] = scale
        table[node, CORE] = node & 1
    return table.astype(np.float32)


class Plane:
    def __init__(self, ref, *index):
        self.ref, self.index = ref, index

    def rows(self, first, count):
        return self.ref[(*self.index, pl.ds(first, count))]

    def put(self, first, value):
        self.ref[(*self.index, pl.ds(first, value.shape[0]))] = value


def flat_sum(plane, first, count):
    whole = plane.ref.shape[-2]
    centre = plane.rows(first, count)
    above, below = plane.rows((first - 8) % whole, 8), plane.rows((first + count) % whole, 8)
    longer = jnp.concatenate([above, centre, below], axis=0)
    vertical = pltpu.roll(longer, 1, 0)[8 : 8 + count] + pltpu.roll(longer, count + 15, 0)[8 : 8 + count]
    columns = centre.shape[1]
    return vertical + (pltpu.roll(centre, 1, 1) + pltpu.roll(centre, columns - 1, 1)), centre


def around(outside, plane, inside, first, count):
    flat, centre = flat_sum(plane, first, count)
    return (outside.rows(first, count) + inside.rows(first, count)) + flat, centre


def chunks(plane, count):
    return range(0, plane.ref.shape[-2], count)


def mixed(scalars, base, planes):
    own, across, beside, corner = (scalars[base + index] * plane for index, plane in enumerate(planes))
    return (own + across) + (beside + corner)


def cubed(state):
    return state - state * state * state


def counter(scalars):
    upper = (scalars[CORE] > 0.5).astype(jnp.int32)
    base, sign = upper * (SLAB - 1), 1 - 2 * upper
    return lambda place: base + sign * (place - OUTER)


def send_kernel(scalars, own, beside, halo_a, halo_b):
    plane = counter(scalars)
    for number, source in enumerate((own, beside)):
        for index in range(3):
            halo_a[index + 3 * number] = source[plane(10 + index)]
        for index in range(2):
            halo_b[index + 2 * number] = source[plane(8 + index)]


def end_kernel(scalars, own, across, beside, corner, start, out, total):
    plane = counter(scalars)
    sources = (own, across, beside, corner)
    weighted = [Plane(total, index) for index in range(HALF + 2)]

    def states(place, first):
        return [Plane(source, plane(place)).rows(first, 32) for source in sources]

    for first in chunks(weighted[0], 32):
        weighted[0].put(first, jnp.zeros_like(weighted[0].rows(first, 32)))
        for index in range(1, HALF + 2):
            value = mixed(scalars, WEIGHT, states(index + 4, first))
            weighted[index].put(first, value)
            if index == 1:
                Plane(out, 0).put(first, (time_step * diffusion) * value)
    for index in range(1, HALF + 1):
        place = index + 4
        for first in chunks(weighted[0], 32):
            local = mixed(scalars, WEIGHT, [cubed(state) for state in states(place, first)])
            nearby, centre = around(*weighted[index - 1 : index + 2], first, 32)
            force = diffusion * (nearby - 6.0 * centre) + reaction * local
            Plane(out, index).put(first, Plane(start, plane(place)).rows(first, 32) + time_step * force)


NAMES = ("g", "x1", "x2", "x3", "x4")
STAGES = [
    {"g": range(6, 12), "x1": range(6, 12), "x2": range(7, 11), "x3": range(8, 10), "x4": ()},
    {"g": range(3, 6), "x1": range(3, 6), "x2": range(4, 7), "x3": range(5, 8), "x4": range(6, 9)},
    {"g": range(1, 3), "x1": range(1, 3), "x2": range(2, 4), "x3": range(3, 5), "x4": range(4, 6)},
]
KEPT = [
    {"g": (6, 7, 8), "x1": (6, 7), "x2": (7, 8), "x3": (8, 9), "x4": ()},
    {"g": (3, 4, 5), "x1": (3, 4), "x2": (4, 5), "x3": (5, 6), "x4": (6, 7, 8)},
    {"g": (), "x1": (), "x2": (), "x3": (), "x4": (4, 5)},
]


def kept_keys(stage):
    return [(name, place) for name in NAMES for place in KEPT[stage][name]]


def spare_keys(stage):
    return [(name, place) for name in NAMES for place in STAGES[stage][name] if place not in KEPT[stage][name]]


def run_stage(stage, scalars, state, old, out, spare):
    where = {}
    for ref, keys in ((old, kept_keys(stage - 1) if stage else []), (out, kept_keys(stage)), (spare, spare_keys(stage))):
        where.update({key: (ref, index) for index, key in enumerate(keys)})

    def plane(name, target, place):
        ref, index = where[name, place]
        return Plane(ref, target, index)

    targets = range(NODES)
    for place in STAGES[stage]["g"]:
        sources = [[state(source, place + by) for by in (-1, 0, 1)] for source in range(NODES)]
        for first in chunks(sources[0][0], RIGHT_ROWS):
            nearby, centre = zip(*(around(*planes, first, RIGHT_ROWS) for planes in sources))
            spread_ = [value - 6.0 * middle for value, middle in zip(nearby, centre)]
            local = [cubed(middle) for middle in centre]
            for target in targets:
                value = mixed(scalars, LIN + 4 * target, spread_) + mixed(scalars, CUB + 4 * target, local)
                plane("g", target, place).put(first, value)
                plane("x1", target, place).put(first, value + scalars[MIX + target] * nearby[target])
    for name, before in (("x2", "x1"), ("x3", "x2"), ("x4", "x3")):
        for place in STAGES[stage][name]:
            for target in targets:
                planes = [plane(before, target, place + by) for by in (-1, 0, 1)]
                base, sink = plane("g", target, place), plane(name, target, place)
                for first in chunks(sink, PASS_ROWS):
                    nearby, _ = around(*planes, first, PASS_ROWS)
                    sink.put(first, base.rows(first, PASS_ROWS) + scalars[MIX + target] * nearby)


def first_kernel(scalars, own, across, beside, corner, out, spare):
    plane = counter(scalars)
    sources = (own, across, beside, corner)
    run_stage(0, scalars, lambda source, place: Plane(sources[source], plane(place)), None, out, spare)


def halo_state(halo, halo_across, first, count):
    def state(source, place):
        ref = (halo, halo_across, halo, halo_across)[source]
        return Plane(ref, (count if source >= 2 else 0) + place - first)

    return state


def second_kernel(scalars, own, across, beside, corner, halo_a, across_a, kept, out, spare):
    plane = counter(scalars)
    sources = (own, across, beside, corner)
    outer = halo_state(halo_a, across_a, 2, 3)

    def state(source, place):
        return outer(source, place) if place < OUTER else Plane(sources[source], plane(place))

    run_stage(1, scalars, state, kept, out, spare)


def third_kernel(scalars, halo_a, across_a, halo_b, across_b, kept, out, spare):
    inner, outer = halo_state(halo_a, across_a, 2, 3), halo_state(halo_b, across_b, 0, 2)

    def state(source, place):
        return outer(source, place) if place < 2 else inner(source, place)

    run_stage(2, scalars, state, kept, out, spare)


def around_place(ref, place, first, count):
    return around(*(Plane(ref, place + by) for by in (-1, 0, 1)), first, count)


def raise_power(source, sink, places):
    for place in places:
        out = Plane(sink, place)
        for first in chunks(out, 32):
            out.put(first, around_place(source, place, first, 32)[0])


def begin_kernel(scalars, start, halo_start, near, away, begin, once, twice):
    plane = counter(scalars)
    begin_first = scalars[FIRST]
    back = (scalars[CORE] > 0.5).astype(jnp.int32)
    for place in range(1, 5):
        begin[place] = halo_start[place - 1 + back * (5 - 2 * place)] + away[5 - place]
    begin[4] = begin[4] + near[0]
    begin[5] = (begin_first * start[plane(5)] + near[1]) + away[0]
    for place in range(6, 9):
        begin[place] = begin_first * start[plane(place)] + near[place - 4]
    raise_power(begin, once, range(2, 8))
    raise_power(once, twice, range(3, 7))


def last_kernel(
    scalars, start, far, begin_near, once_near, twice_near, kept, part, mine, swap, begin, once, twice, last, total
):
    plane = counter(scalars)
    begin_first = scalars[FIRST]
    for place in range(9, 12):
        begin[place] = begin_first * start[plane(place)] + far[11 - place]

    def at(place, near, own, split):
        return Plane(near if place < split else own, place)

    def raised(near_source, source, split, sink, places):
        for place in places:
            planes = [at(place + by, near_source, source, split) for by in (-1, 0, 1)]
            out = Plane(sink, place)
            for first in chunks(out, 32):
                out.put(first, around(*planes, first, 32)[0])

    raised(begin_near, begin, 9, once, range(8, 11))
    raised(once_near, once, 8, twice, range(7, 10))
    kept_x4 = {key: index for index, key in enumerate(kept_keys(1))}
    for place in range(4, 9):
        planes = [at(place + by, twice_near, twice, 7) for by in (-1, 0, 1)]
        for first in chunks(Plane(total, 0), 16):
            thrice, two = around(*planes, first, 16)
            zero, one = Plane(begin_near, place).rows(first, 16), at(place, once_near, once, 8).rows(first, 16)
            values = []
            for target in range(NODES):
                mix = scalars[MIX + target]
                rest = Plane(part, target, place - 4) if place < 6 else Plane(kept, target, kept_x4["x4", place])
                value = scalars[SCALE + target] * (zero + mix * (one + mix * (two + mix * thrice)))
                values.append(rest.rows(first, 16) + value)
                Plane(last, target, place - 4).put(first, values[-1])
            Plane(total, place - 4).put(first, mixed(scalars, WEIGHT, values))
    total[5] = jnp.zeros_like(total[5])
    for place in range(OUTER, OUTER + HALF):
        index = place - 4
        for first in chunks(Plane(total, 0), 16):
            states = [Plane(last, target, index).rows(first, 16) for target in range(NODES)]
            local = mixed(scalars, WEIGHT, [cubed(state) for state in states])
            nearby, centre = around_place(total, index, first, 16)
            force = diffusion * (nearby - 6.0 * centre) + reaction * local
            Plane(mine, index - 1).put(first, states[0])
            Plane(swap, index - 1).put(first, states[2])
            Plane(swap, index - 1 + HALF).put(first, Plane(begin_near, place).rows(first, 16) + time_step * force)
    swap[2 * HALF] = total[HALF]


def join_kernel(scalars, mine, swap, other, state, end):
    plane = counter(scalars)
    for index in range(HALF):
        near, far = plane(OUTER + index), plane(OUTER + SLAB - 1 - index)
        state[near] = mine[index]
        state[far] = other[index]
        own, others = swap[HALF + index], other[HALF + index]
        if index == HALF - 1:
            own = own + (time_step * diffusion) * other[2 * HALF]
            others = others + (time_step * diffusion) * swap[2 * HALF]
        end[near] = own
        end[far] = others


def call(kernel, scalars, operands, outs, scratch, limit):
    return pl.pallas_call(
        kernel,
        out_shape=[jax.ShapeDtypeStruct(shape, F32) for shape in outs],
        in_specs=[pl.BlockSpec(memory_space=pltpu.SMEM)] + [pl.BlockSpec(memory_space=pltpu.VMEM)] * len(operands),
        out_specs=[pl.BlockSpec(memory_space=pltpu.VMEM)] * len(outs),
        scratch_shapes=[pltpu.VMEM(shape, F32) for shape in scratch],
        compiler_params=pltpu.CompilerParams(vmem_limit_bytes=limit << 20),
        cost_estimate=pl.CostEstimate(flops=1000, bytes_accessed=1000, transcendentals=0),
    )(scalars, *operands)


def on_device(start_old, nodes_old):
    slabs, slices = lax.axis_size("space"), lax.axis_size("tm")
    node_index = lax.axis_index("node")
    slice_index = lax.axis_index("tm")
    state, start = nodes_old[0, 0], start_old[0]
    slab, rows, columns = state.shape
    scalars = jnp.asarray(scalar_table())[node_index]
    scalars = scalars.at[FIRST].set((slice_index == 0).astype(F32))

    def after(array, other):
        return lax.optimization_barrier((array, other))[0]

    def planes(*lead):
        return (*lead, rows, columns)

    def across(array):
        return lax.ppermute(array, "node", [(node, node ^ 2) for node in range(NODES)])

    def beside(array):
        return lax.ppermute(array, "node", [(node, node ^ 1) for node in range(NODES)])

    always = scalars[WEIGHT] > 0.0

    def swapped(array):
        return lax.cond(always, beside, lambda array: array, array)

    def device(slab_, node, slice_):
        return ((slab_ % slabs) * NODES + node) * slices + slice_

    def spread(array, steps, by, flip=0):
        pairs = [
            (device(slab_, node, here), device(slab_ + by[node % 2], node ^ flip, there))
            for slab_ in range(slabs) for node in range(NODES) for here, there in steps
        ]
        return lax.ppermute(array, ("space", "node", "tm"), pairs)

    same = [(slice_, slice_) for slice_ in range(slices)]
    onward = [(slice_, slice_ + 1) for slice_ in range(slices - 1)]

    beside_state = beside(state)
    across_state = across(state)
    send_a, send_b = call(send_kernel, scalars, [state, beside_state], [planes(6), planes(4)], [], 16)
    halo_a = spread(send_a, same, (1, -1))
    halo_b = spread(send_b, same, (1, -1))
    corner_state = swapped(after(across_state, send_a))
    sources = [state, across_state, beside_state, corner_state]
    first_start = lax.dynamic_slice_in_dim(start, HALF * (1 - lax.rem(node_index, 2)), HALF, axis=0)
    passing_start = spread(first_start, [(0, 1)], (0, 0))
    (send_end,) = call(
        end_kernel, scalars, [*sources, after(start, passing_start)], [planes(5)], [planes(HALF + 2)], 16
    )
    near = spread(send_end, onward, (0, 0))
    away = spread(send_end, onward, (-1, 1), 1)
    across_a = across(after(halo_a, corner_state))
    halo_start = spread(passing_start, [(1, 0)], (1, -1))

    def stage(index, kernel, operands, limit):
        shapes = [planes(NODES, len(keys)) for keys in (kept_keys(index), spare_keys(index))]
        return call(kernel, scalars, operands, shapes[:1], shapes[1:], limit)[0]

    kept = stage(0, first_kernel, sources, 24)
    across_b = across(after(halo_b, kept))
    kept = stage(1, second_kernel, [*sources, halo_a, across_a, kept], 24)
    part = stage(2, third_kernel, [halo_a, across_a, halo_b, across_b, kept], 24)
    far = beside(after(near, part)[2:])
    begun = call(begin_kernel, scalars, [start, halo_start, near, away], [planes(9), planes(8), planes(7)], [], 16)
    mine, swap = call(
        last_kernel, scalars, [start, far, *begun, kept, part], [planes(HALF), planes(2 * HALF + 1)],
        [planes(12), planes(11), planes(10), planes(NODES, 5), planes(6)], 24,
    )
    state_new, end_new = call(join_kernel, scalars, [mine, swap, beside(swap)], [planes(slab)] * 2, [], 16)
    return (state_new[None, None], end_new[None])


def solution(mesh):
    return jax.shard_map(
        on_device,
        mesh=mesh,
        in_specs=(P("tm", "space", None, None), P("tm", "node", "space", None, None)),
        out_specs=(P("tm", "node", "space", None, None), P("tm", "space", None, None)),
        check_vma=False,
    )
```

```python
import functools

import jax
import jax.numpy as jnp
import numpy as np
from jax import lax
from jax.experimental import pallas as pl
from jax.experimental.pallas import tpu as pltpu
from jax.sharding import PartitionSpec as P

NODES = 4
PASSES = 4

time_step = 0.25
diffusion = 4.0
reaction = 1.0

F32 = jnp.float32

OUTER = 5
SLAB = 8
HALF = 4
RIGHT_ROWS, PASS_ROWS = 16, 32


def collocation(count):
    points = [-0.8611363115940526, -0.3399810435848563, 0.3399810435848563, 0.8611363115940526]
    raw_weights = [0.3478548451374538, 0.6521451548625461, 0.6521451548625461, 0.3478548451374538]
    node_times = [(point + 1.0) / 2.0 for point in points]
    quadrature = [[0.0 for column in range(count)] for target in range(count)]
    for source in range(count):
        coeffs = [1.0]
        scaling = 1.0
        for other in range(count):
            if other != source:
                other_time = node_times[other]
                shifted = [0.0] + coeffs
                for power in range(len(coeffs)):
                    shifted[power] = shifted[power] - other_time * coeffs[power]
                coeffs = shifted
                scaling = scaling * (node_times[source] - other_time)
        for target in range(count):
            target_time = node_times[target]
            integral = 0.0
            for power in range(len(coeffs)):
                integral = integral + coeffs[power] * target_time ** (power + 1) / (power + 1)
            quadrature[target][source] = integral / scaling
    return (node_times, quadrature, [weight / 2.0 for weight in raw_weights])


LIN, CUB, WEIGHT, MIX, SCALE, FIRST, CORE, COUNT = 0, 16, 32, 36, 40, 44, 45, 46


def scalar_table():
    times, quad, weights = collocation(NODES)
    table = np.zeros((NODES, COUNT), np.float64)
    for node in range(NODES):
        order = [node, node ^ 2, node ^ 1, node ^ 3]
        for place, target in enumerate(order):
            implicit = time_step * diffusion * times[target]
            scale = 1.0 / (1.0 + 6.0 * implicit)
            for index, source in enumerate(order):
                lin = time_step * diffusion * quad[target][source] - (implicit if source == target else 0.0)
                table[node, LIN + 4 * place + index] = scale * lin
                table[node, CUB + 4 * place + index] = scale * time_step * reaction * quad[target][source]
            table[node, WEIGHT + place] = weights[target]
            table[node, MIX + place] = scale * implicit
            table[node, SCALE + place] = scale
        table[node, CORE] = node & 1
    return table.astype(np.float32)


class Plane:
    def __init__(self, ref, *index):
        self.ref, self.index = ref, index

    def rows(self, first, count):
        return self.ref[(*self.index, pl.ds(first, count))]

    def put(self, first, value):
        self.ref[(*self.index, pl.ds(first, value.shape[0]))] = value


def flat_sum(plane, first, count):
    whole = plane.ref.shape[-2]
    centre = plane.rows(first, count)
    above, below = plane.rows((first - 8) % whole, 8), plane.rows((first + count) % whole, 8)
    longer = jnp.concatenate([above, centre, below], axis=0)
    vertical = pltpu.roll(longer, 1, 0)[8 : 8 + count] + pltpu.roll(longer, count + 15, 0)[8 : 8 + count]
    columns = centre.shape[1]
    return vertical + (pltpu.roll(centre, 1, 1) + pltpu.roll(centre, columns - 1, 1)), centre


def around(outside, plane, inside, first, count):
    flat, centre = flat_sum(plane, first, count)
    return (outside.rows(first, count) + inside.rows(first, count)) + flat, centre


def chunks(plane, count):
    return range(0, plane.ref.shape[-2], count)


def mixed(scalars, base, planes):
    own, across, beside, corner = (scalars[base + index] * plane for index, plane in enumerate(planes))
    return (own + across) + (beside + corner)


def cubed(state):
    return state - state * state * state


def counter(scalars):
    upper = (scalars[CORE] > 0.5).astype(jnp.int32)
    base, sign = upper * (SLAB - 1), 1 - 2 * upper
    return lambda place: base + sign * (place - OUTER)


def send_kernel(scalars, own, beside, halo_a, halo_b):
    plane = counter(scalars)
    for number, source in enumerate((own, beside)):
        for index in range(3):
            halo_a[index + 3 * number] = source[plane(10 + index)]
        for index in range(2):
            halo_b[index + 2 * number] = source[plane(8 + index)]


def end_kernel(scalars, own, across, beside, corner, start, out, total):
    plane = counter(scalars)
    sources = (own, across, beside, corner)
    weighted = [Plane(total, index) for index in range(HALF + 2)]

    def states(place, first):
        return [Plane(source, plane(place)).rows(first, 32) for source in sources]

    for first in chunks(weighted[0], 32):
        weighted[0].put(first, jnp.zeros_like(weighted[0].rows(first, 32)))
        for index in range(1, HALF + 2):
            value = mixed(scalars, WEIGHT, states(index + 4, first))
            weighted[index].put(first, value)
            if index == 1:
                Plane(out, 0).put(first, (time_step * diffusion) * value)
    for index in range(1, HALF + 1):
        place = index + 4
        for first in chunks(weighted[0], 32):
            local = mixed(scalars, WEIGHT, [cubed(state) for state in states(place, first)])
            nearby, centre = around(*weighted[index - 1 : index + 2], first, 32)
            force = diffusion * (nearby - 6.0 * centre) + reaction * local
            Plane(out, index).put(first, Plane(start, plane(place)).rows(first, 32) + time_step * force)


NAMES = ("g", "x1", "x2", "x3", "x4")
STAGES = [
    {"g": range(6, 12), "x1": range(6, 12), "x2": range(7, 11), "x3": range(8, 10), "x4": ()},
    {"g": range(3, 6), "x1": range(3, 6), "x2": range(4, 7), "x3": range(5, 8), "x4": range(6, 9)},
    {"g": range(1, 3), "x1": range(1, 3), "x2": range(2, 4), "x3": range(3, 5), "x4": range(4, 6)},
]
KEPT = [
    {"g": (6, 7, 8), "x1": (6, 7), "x2": (7, 8), "x3": (8, 9), "x4": ()},
    {"g": (3, 4, 5), "x1": (3, 4), "x2": (4, 5), "x3": (5, 6), "x4": (6, 7, 8)},
    {"g": (), "x1": (), "x2": (), "x3": (), "x4": (4, 5)},
]


def kept_keys(stage):
    return [(name, place) for name in NAMES for place in KEPT[stage][name]]


def spare_keys(stage):
    return [(name, place) for name in NAMES for place in STAGES[stage][name] if place not in KEPT[stage][name]]


def run_stage(stage, scalars, state, old, out, spare):
    where = {}
    for ref, keys in ((old, kept_keys(stage - 1) if stage else []), (out, kept_keys(stage)), (spare, spare_keys(stage))):
        where.update({key: (ref, index) for index, key in enumerate(keys)})

    def plane(name, target, place):
        ref, index = where[name, place]
        return Plane(ref, target, index)

    targets = range(NODES)
    for place in STAGES[stage]["g"]:
        sources = [[state(source, place + by) for by in (-1, 0, 1)] for source in range(NODES)]
        for first in chunks(sources[0][0], RIGHT_ROWS):
            nearby, centre = zip(*(around(*planes, first, RIGHT_ROWS) for planes in sources))
            spread_ = [value - 6.0 * middle for value, middle in zip(nearby, centre)]
            local = [cubed(middle) for middle in centre]
            for target in targets:
                value = mixed(scalars, LIN + 4 * target, spread_) + mixed(scalars, CUB + 4 * target, local)
                plane("g", target, place).put(first, value)
                plane("x1", target, place).put(first, value + scalars[MIX + target] * nearby[target])
    for name, before in (("x2", "x1"), ("x3", "x2"), ("x4", "x3")):
        for place in STAGES[stage][name]:
            for target in targets:
                planes = [plane(before, target, place + by) for by in (-1, 0, 1)]
                base, sink = plane("g", target, place), plane(name, target, place)
                for first in chunks(sink, PASS_ROWS):
                    nearby, _ = around(*planes, first, PASS_ROWS)
                    sink.put(first, base.rows(first, PASS_ROWS) + scalars[MIX + target] * nearby)


def first_kernel(scalars, own, across, beside, corner, out, spare):
    plane = counter(scalars)
    sources = (own, across, beside, corner)
    run_stage(0, scalars, lambda source, place: Plane(sources[source], plane(place)), None, out, spare)


def halo_state(halo, halo_across, first, count):
    def state(source, place):
        ref = (halo, halo_across, halo, halo_across)[source]
        return Plane(ref, (count if source >= 2 else 0) + place - first)

    return state


def second_kernel(scalars, own, across, beside, corner, halo_a, across_a, kept, out, spare):
    plane = counter(scalars)
    sources = (own, across, beside, corner)
    outer = halo_state(halo_a, across_a, 2, 3)

    def state(source, place):
        return outer(source, place) if place < OUTER else Plane(sources[source], plane(place))

    run_stage(1, scalars, state, kept, out, spare)


def third_kernel(scalars, halo_a, across_a, halo_b, across_b, kept, out, spare):
    inner, outer = halo_state(halo_a, across_a, 2, 3), halo_state(halo_b, across_b, 0, 2)

    def state(source, place):
        return outer(source, place) if place < 2 else inner(source, place)

    run_stage(2, scalars, state, kept, out, spare)


def around_place(ref, place, first, count):
    return around(*(Plane(ref, place + by) for by in (-1, 0, 1)), first, count)


def raise_power(source, sink, places):
    for place in places:
        out = Plane(sink, place)
        for first in chunks(out, 32):
            out.put(first, around_place(source, place, first, 32)[0])


def begin_kernel(scalars, start, halo_start, near, away, begin, once, twice):
    plane = counter(scalars)
    begin_first = scalars[FIRST]
    back = (scalars[CORE] > 0.5).astype(jnp.int32)
    for place in range(1, 5):
        begin[place] = halo_start[place - 1 + back * (5 - 2 * place)] + away[5 - place]
    begin[4] = begin[4] + near[0]
    begin[5] = (begin_first * start[plane(5)] + near[1]) + away[0]
    for place in range(6, 9):
        begin[place] = begin_first * start[plane(place)] + near[place - 4]
    raise_power(begin, once, range(2, 8))
    raise_power(once, twice, range(3, 7))


def last_kernel(
    scalars, start, far, begin_near, once_near, twice_near, kept, part, mine, swap, begin, once, twice, last, total
):
    plane = counter(scalars)
    begin_first = scalars[FIRST]
    back = (scalars[CORE] > 0.5).astype(jnp.int32)
    for place in range(9, 12):
        begin[place] = begin_first * start[plane(place)] + far[11 - place]

    def at(place, near, own, split):
        return Plane(near if place < split else own, place)

    def raised(near_source, source, split, sink, places):
        for place in places:
            planes = [at(place + by, near_source, source, split) for by in (-1, 0, 1)]
            out = Plane(sink, place)
            for first in chunks(out, 32):
                out.put(first, around(*planes, first, 32)[0])

    raised(begin_near, begin, 9, once, range(8, 11))
    raised(once_near, once, 8, twice, range(7, 10))
    kept_x4 = {key: index for index, key in enumerate(kept_keys(1))}
    for place in range(4, 9):
        planes = [at(place + by, twice_near, twice, 7) for by in (-1, 0, 1)]
        for first in chunks(Plane(total, 0), 16):
            thrice, two = around(*planes, first, 16)
            zero, one = Plane(begin_near, place).rows(first, 16), at(place, once_near, once, 8).rows(first, 16)
            values = []
            for target in range(NODES):
                mix = scalars[MIX + target]
                rest = Plane(part, target, place - 4) if place < 6 else Plane(kept, target, kept_x4["x4", place])
                value = scalars[SCALE + target] * (zero + mix * (one + mix * (two + mix * thrice)))
                values.append(rest.rows(first, 16) + value)
                Plane(last, target, place - 4).put(first, values[-1])
            Plane(total, place - 4).put(first, mixed(scalars, WEIGHT, values))
    total[5] = jnp.zeros_like(total[5])
    for place in range(OUTER, OUTER + HALF):
        index = place - 4
        order = index - 1 + back * (HALF + 1 - 2 * index)
        for first in chunks(Plane(total, 0), 16):
            states = [Plane(last, target, index).rows(first, 16) for target in range(NODES)]
            local = mixed(scalars, WEIGHT, [cubed(state) for state in states])
            nearby, centre = around_place(total, index, first, 16)
            force = diffusion * (nearby - 6.0 * centre) + reaction * local
            Plane(mine, order).put(first, states[0])
            Plane(swap, order).put(first, states[2])
            Plane(swap, order + HALF).put(first, Plane(begin_near, place).rows(first, 16) + time_step * force)
    swap[2 * HALF] = total[HALF]


def finished(copies):
    for copy in copies:
        copy.start()
    for copy in copies:
        copy.wait()


def own_half_kernel(scalars, mine, swap, state, end, sems):
    upper = (scalars[CORE] > 0.5).astype(jnp.int32)
    base = HALF * upper
    inner = pl.ds(HALF + upper, HALF - 1)
    finished([
        pltpu.make_async_copy(mine, state.at[pl.ds(base, HALF)], sems.at[0]),
        pltpu.make_async_copy(swap.at[inner], end.at[pl.ds(base + upper, HALF - 1)], sems.at[1]),
    ])


def other_half_kernel(scalars, swap, other, state_before, end_before, state, end, cut, sems):
    upper = (scalars[CORE] > 0.5).astype(jnp.int32)
    base, base_other = HALF * upper, HALF * (1 - upper)
    edge, edge_other = (HALF - 1) * (1 - upper), (HALF - 1) * upper
    inner = pl.ds(HALF + 1 - upper, HALF - 1)
    halves = [
        pltpu.make_async_copy(other.at[pl.ds(0, HALF)], state.at[pl.ds(base_other, HALF)], sems.at[0]),
        pltpu.make_async_copy(other.at[inner], end.at[pl.ds(base_other + 1 - upper, HALF - 1)], sems.at[1]),
    ]
    for copy in halves:
        copy.start()
    cut[0] = swap[HALF + edge] + (time_step * diffusion) * other[2 * HALF]
    cut[1] = other[HALF + edge_other] + (time_step * diffusion) * swap[2 * HALF]
    finished([
        pltpu.make_async_copy(cut.at[0], end.at[base + edge], sems.at[2]),
        pltpu.make_async_copy(cut.at[1], end.at[base_other + edge_other], sems.at[3]),
    ])
    for copy in halves:
        copy.wait()


def join_call(scalars, mine, swap, other, shape):
    def placed(kernel, operands, before, scratch, sems):
        vmem, anywhere = pl.BlockSpec(memory_space=pltpu.VMEM), pl.BlockSpec(memory_space=pl.ANY)
        first = 1 + len(operands)
        return pl.pallas_call(
            kernel,
            out_shape=[jax.ShapeDtypeStruct(shape, F32)] * 2,
            in_specs=[pl.BlockSpec(memory_space=pltpu.SMEM)] + [vmem] * len(operands) + [anywhere] * len(before),
            out_specs=[anywhere] * 2,
            input_output_aliases={first + index: index for index in range(len(before))},
            scratch_shapes=[*scratch, pltpu.SemaphoreType.DMA((sems,))],
            compiler_params=pltpu.CompilerParams(vmem_limit_bytes=16 << 20),
            cost_estimate=pl.CostEstimate(flops=1000, bytes_accessed=1000, transcendentals=0),
        )(scalars, *operands, *before)

    halves = placed(own_half_kernel, [mine, swap], [], [], 2)
    return placed(other_half_kernel, [swap, other], halves, [pltpu.VMEM((2, *shape[1:]), F32)], 4)


def call(kernel, scalars, operands, outs, scratch, limit):
    return pl.pallas_call(
        kernel,
        out_shape=[jax.ShapeDtypeStruct(shape, F32) for shape in outs],
        in_specs=[pl.BlockSpec(memory_space=pltpu.SMEM)] + [pl.BlockSpec(memory_space=pltpu.VMEM)] * len(operands),
        out_specs=[pl.BlockSpec(memory_space=pltpu.VMEM)] * len(outs),
        scratch_shapes=[pltpu.VMEM(shape, F32) for shape in scratch],
        compiler_params=pltpu.CompilerParams(vmem_limit_bytes=limit << 20),
        cost_estimate=pl.CostEstimate(flops=1000, bytes_accessed=1000, transcendentals=0),
    )(scalars, *operands)


def on_device(start_old, nodes_old):
    slabs, slices = lax.axis_size("space"), lax.axis_size("tm")
    node_index = lax.axis_index("node")
    slice_index = lax.axis_index("tm")
    state, start = nodes_old[0, 0], start_old[0]
    slab, rows, columns = state.shape
    scalars = jnp.asarray(scalar_table())[node_index]
    scalars = scalars.at[FIRST].set((slice_index == 0).astype(F32))

    def after(array, other):
        return lax.optimization_barrier((array, other))[0]

    def planes(*lead):
        return (*lead, rows, columns)

    def across(array):
        return lax.ppermute(array, "node", [(node, node ^ 2) for node in range(NODES)])

    def beside(array):
        return lax.ppermute(array, "node", [(node, node ^ 1) for node in range(NODES)])

    always = scalars[WEIGHT] > 0.0

    def swapped(array):
        return lax.cond(always, beside, lambda array: array, array)

    def device(slab_, node, slice_):
        return ((slab_ % slabs) * NODES + node) * slices + slice_

    def spread(array, steps, by, flip=0):
        pairs = [
            (device(slab_, node, here), device(slab_ + by[node % 2], node ^ flip, there))
            for slab_ in range(slabs) for node in range(NODES) for here, there in steps
        ]
        return lax.ppermute(array, ("space", "node", "tm"), pairs)

    same = [(slice_, slice_) for slice_ in range(slices)]
    onward = [(slice_, slice_ + 1) for slice_ in range(slices - 1)]

    beside_state = beside(state)
    across_state = across(state)
    send_a, send_b = call(send_kernel, scalars, [state, beside_state], [planes(6), planes(4)], [], 16)
    halo_a = spread(send_a, same, (1, -1))
    halo_b = spread(send_b, same, (1, -1))
    corner_state = swapped(after(across_state, send_a))
    sources = [state, across_state, beside_state, corner_state]
    first_start = lax.dynamic_slice_in_dim(start, HALF * (1 - lax.rem(node_index, 2)), HALF, axis=0)
    passing_start = spread(first_start, [(0, 1)], (0, 0))
    (send_end,) = call(
        end_kernel, scalars, [*sources, after(start, passing_start)], [planes(5)], [planes(HALF + 2)], 16
    )
    near = spread(send_end, onward, (0, 0))
    away = spread(send_end, onward, (-1, 1), 1)
    across_a = across(after(halo_a, corner_state))
    halo_start = spread(passing_start, [(1, 0)], (1, -1))

    def stage(index, kernel, operands, limit):
        shapes = [planes(NODES, len(keys)) for keys in (kept_keys(index), spare_keys(index))]
        return call(kernel, scalars, operands, shapes[:1], shapes[1:], limit)[0]

    kept = stage(0, first_kernel, sources, 24)
    across_b = across(after(halo_b, kept))
    kept = stage(1, second_kernel, [*sources, halo_a, across_a, kept], 24)
    part = stage(2, third_kernel, [halo_a, across_a, halo_b, across_b, kept], 24)
    far = beside(after(near, part)[2:])
    begun = call(begin_kernel, scalars, [start, halo_start, near, away], [planes(9), planes(8), planes(7)], [], 16)
    mine, swap = call(
        last_kernel, scalars, [start, far, *begun, kept, part], [planes(HALF), planes(2 * HALF + 1)],
        [planes(12), planes(11), planes(10), planes(NODES, 5), planes(6)], 24,
    )
    state_new, end_new = join_call(scalars, mine, swap, beside(swap), planes(slab))
    return (state_new[None, None], end_new[None])


def solution(mesh):
    return jax.shard_map(
        on_device,
        mesh=mesh,
        in_specs=(P("tm", "space", None, None), P("tm", "node", "space", None, None)),
        out_specs=(P("tm", "node", "space", None, None), P("tm", "space", None, None)),
        check_vma=False,
    )
```

```python
import functools

import jax
import jax.numpy as jnp
import numpy as np
from jax import lax
from jax.experimental import pallas as pl
from jax.experimental.pallas import tpu as pltpu
from jax.sharding import PartitionSpec as P

NODES = 4
PASSES = 4

time_step = 0.25
diffusion = 4.0
reaction = 1.0

F32 = jnp.float32

OUTER = 5
SLAB = 8
HALF = 4
RIGHT_ROWS, PASS_ROWS = 16, 32


def collocation(count):
    points = [-0.8611363115940526, -0.3399810435848563, 0.3399810435848563, 0.8611363115940526]
    raw_weights = [0.3478548451374538, 0.6521451548625461, 0.6521451548625461, 0.3478548451374538]
    node_times = [(point + 1.0) / 2.0 for point in points]
    quadrature = [[0.0 for column in range(count)] for target in range(count)]
    for source in range(count):
        coeffs = [1.0]
        scaling = 1.0
        for other in range(count):
            if other != source:
                other_time = node_times[other]
                shifted = [0.0] + coeffs
                for power in range(len(coeffs)):
                    shifted[power] = shifted[power] - other_time * coeffs[power]
                coeffs = shifted
                scaling = scaling * (node_times[source] - other_time)
        for target in range(count):
            target_time = node_times[target]
            integral = 0.0
            for power in range(len(coeffs)):
                integral = integral + coeffs[power] * target_time ** (power + 1) / (power + 1)
            quadrature[target][source] = integral / scaling
    return (node_times, quadrature, [weight / 2.0 for weight in raw_weights])


LIN, CUB, WEIGHT, MIX, SCALE, FIRST, CORE, COUNT = 0, 16, 32, 36, 40, 44, 45, 46


def scalar_table():
    times, quad, weights = collocation(NODES)
    table = np.zeros((NODES, COUNT), np.float64)
    for node in range(NODES):
        order = [node, node ^ 2, node ^ 1, node ^ 3]
        for place, target in enumerate(order):
            implicit = time_step * diffusion * times[target]
            scale = 1.0 / (1.0 + 6.0 * implicit)
            for index, source in enumerate(order):
                lin = time_step * diffusion * quad[target][source] - (implicit if source == target else 0.0)
                table[node, LIN + 4 * place + index] = scale * lin
                table[node, CUB + 4 * place + index] = scale * time_step * reaction * quad[target][source]
            table[node, WEIGHT + place] = weights[target]
            table[node, MIX + place] = scale * implicit
            table[node, SCALE + place] = scale
        table[node, CORE] = node & 1
    return table.astype(np.float32)


class Plane:
    def __init__(self, ref, *index):
        self.ref, self.index = ref, index

    def rows(self, first, count):
        return self.ref[(*self.index, pl.ds(first, count))]

    def put(self, first, value):
        self.ref[(*self.index, pl.ds(first, value.shape[0]))] = value


def flat_sum(plane, first, count):
    whole = plane.ref.shape[-2]
    centre = plane.rows(first, count)
    above, below = plane.rows((first - 8) % whole, 8), plane.rows((first + count) % whole, 8)
    longer = jnp.concatenate([above, centre, below], axis=0)
    vertical = pltpu.roll(longer, 1, 0)[8 : 8 + count] + pltpu.roll(longer, count + 15, 0)[8 : 8 + count]
    columns = centre.shape[1]
    return vertical + (pltpu.roll(centre, 1, 1) + pltpu.roll(centre, columns - 1, 1)), centre


def around(outside, plane, inside, first, count):
    flat, centre = flat_sum(plane, first, count)
    return (outside.rows(first, count) + inside.rows(first, count)) + flat, centre


def chunks(plane, count):
    return range(0, plane.ref.shape[-2], count)


def mixed(scalars, base, planes):
    own, across, beside, corner = (scalars[base + index] * plane for index, plane in enumerate(planes))
    return (own + across) + (beside + corner)


def cubed(state):
    return state - state * state * state


def counter(scalars):
    upper = (scalars[CORE] > 0.5).astype(jnp.int32)
    base, sign = upper * (SLAB - 1), 1 - 2 * upper
    return lambda place: base + sign * (place - OUTER)


def send_kernel(scalars, own, beside, halo_a, halo_b):
    plane = counter(scalars)
    for number, source in enumerate((own, beside)):
        for index in range(3):
            halo_a[index + 3 * number] = source[plane(10 + index)]
        for index in range(2):
            halo_b[index + 2 * number] = source[plane(8 + index)]


def end_kernel(scalars, own, across, beside, corner, start, out, total):
    plane = counter(scalars)
    sources = (own, across, beside, corner)
    weighted = [Plane(total, index) for index in range(HALF + 2)]

    def states(place, first):
        return [Plane(source, plane(place)).rows(first, 32) for source in sources]

    for first in chunks(weighted[0], 32):
        weighted[0].put(first, jnp.zeros_like(weighted[0].rows(first, 32)))
        for index in range(1, HALF + 2):
            value = mixed(scalars, WEIGHT, states(index + 4, first))
            weighted[index].put(first, value)
            if index == 1:
                Plane(out, 0).put(first, (time_step * diffusion) * value)
    for index in range(1, HALF + 1):
        place = index + 4
        for first in chunks(weighted[0], 32):
            local = mixed(scalars, WEIGHT, [cubed(state) for state in states(place, first)])
            nearby, centre = around(*weighted[index - 1 : index + 2], first, 32)
            force = diffusion * (nearby - 6.0 * centre) + reaction * local
            Plane(out, index).put(first, Plane(start, plane(place)).rows(first, 32) + time_step * force)


NAMES = ("g", "x1", "x2", "x3", "x4")
STAGES = [
    {"g": range(6, 12), "x1": range(6, 12), "x2": range(7, 11), "x3": range(8, 10), "x4": ()},
    {"g": range(3, 6), "x1": range(3, 6), "x2": range(4, 7), "x3": range(5, 8), "x4": range(6, 9)},
    {"g": range(1, 3), "x1": range(1, 3), "x2": range(2, 4), "x3": range(3, 5), "x4": range(4, 6)},
]
KEPT = [
    {"g": (6, 7, 8), "x1": (6, 7), "x2": (7, 8), "x3": (8, 9), "x4": ()},
    {"g": (3, 4, 5), "x1": (3, 4), "x2": (4, 5), "x3": (5, 6), "x4": (6, 7, 8)},
    {"g": (), "x1": (), "x2": (), "x3": (), "x4": (4, 5)},
]


def kept_keys(stage):
    return [(name, place) for name in NAMES for place in KEPT[stage][name]]


def spare_keys(stage):
    return [(name, place) for name in NAMES for place in STAGES[stage][name] if place not in KEPT[stage][name]]


def run_stage(stage, scalars, state, old, out, spare):
    where = {}
    for ref, keys in ((old, kept_keys(stage - 1) if stage else []), (out, kept_keys(stage)), (spare, spare_keys(stage))):
        where.update({key: (ref, index) for index, key in enumerate(keys)})

    def plane(name, target, place):
        ref, index = where[name, place]
        return Plane(ref, target, index)

    targets = range(NODES)
    for place in STAGES[stage]["g"]:
        sources = [[state(source, place + by) for by in (-1, 0, 1)] for source in range(NODES)]
        for first in chunks(sources[0][0], RIGHT_ROWS):
            nearby, centre = zip(*(around(*planes, first, RIGHT_ROWS) for planes in sources))
            spread_ = [value - 6.0 * middle for value, middle in zip(nearby, centre)]
            local = [cubed(middle) for middle in centre]
            for target in targets:
                value = mixed(scalars, LIN + 4 * target, spread_) + mixed(scalars, CUB + 4 * target, local)
                plane("g", target, place).put(first, value)
                plane("x1", target, place).put(first, value + scalars[MIX + target] * nearby[target])
    for name, before in (("x2", "x1"), ("x3", "x2"), ("x4", "x3")):
        for place in STAGES[stage][name]:
            for target in targets:
                planes = [plane(before, target, place + by) for by in (-1, 0, 1)]
                base, sink = plane("g", target, place), plane(name, target, place)
                for first in chunks(sink, PASS_ROWS):
                    nearby, _ = around(*planes, first, PASS_ROWS)
                    sink.put(first, base.rows(first, PASS_ROWS) + scalars[MIX + target] * nearby)


def first_kernel(scalars, own, across, beside, corner, out, spare):
    plane = counter(scalars)
    sources = (own, across, beside, corner)
    run_stage(0, scalars, lambda source, place: Plane(sources[source], plane(place)), None, out, spare)


def halo_state(halo, halo_across, first, count):
    def state(source, place):
        ref = (halo, halo_across, halo, halo_across)[source]
        return Plane(ref, (count if source >= 2 else 0) + place - first)

    return state


def second_kernel(scalars, own, across, beside, corner, halo_a, across_a, kept, out, spare):
    plane = counter(scalars)
    sources = (own, across, beside, corner)
    outer = halo_state(halo_a, across_a, 2, 3)

    def state(source, place):
        return outer(source, place) if place < OUTER else Plane(sources[source], plane(place))

    run_stage(1, scalars, state, kept, out, spare)


def third_kernel(scalars, halo_a, across_a, halo_b, across_b, kept, out, spare):
    inner, outer = halo_state(halo_a, across_a, 2, 3), halo_state(halo_b, across_b, 0, 2)

    def state(source, place):
        return outer(source, place) if place < 2 else inner(source, place)

    run_stage(2, scalars, state, kept, out, spare)


def last_kernel(scalars, start, halo_start, near, far, away, kept, part, mine, swap, begin, once, twice, last, total):
    plane = counter(scalars)
    begin_first = scalars[FIRST]
    back = (scalars[CORE] > 0.5).astype(jnp.int32)
    for place in range(1, 5):
        begin[place] = halo_start[place - 1 + back * (5 - 2 * place)] + away[5 - place]
    begin[4] = begin[4] + near[0]
    begin[5] = (begin_first * start[plane(5)] + near[1]) + away[0]
    for place in range(6, 9):
        begin[place] = begin_first * start[plane(place)] + near[place - 4]
    for place in range(9, 12):
        begin[place] = begin_first * start[plane(place)] + far[11 - place]

    def around_place(ref, place, first, count):
        return around(*(Plane(ref, place + by) for by in (-1, 0, 1)), first, count)

    for source, sink, places in ((begin, once, range(2, 11)), (once, twice, range(3, 10))):
        for place in places:
            out = Plane(sink, place)
            for first in chunks(out, 32):
                out.put(first, around_place(source, place, first, 32)[0])
    kept_x4 = {key: index for index, key in enumerate(kept_keys(1))}
    for place in range(4, 9):
        for first in chunks(Plane(total, 0), 16):
            thrice, two = around_place(twice, place, first, 16)
            zero, one = Plane(begin, place).rows(first, 16), Plane(once, place).rows(first, 16)
            values = []
            for target in range(NODES):
                mix = scalars[MIX + target]
                rest = Plane(part, target, place - 4) if place < 6 else Plane(kept, target, kept_x4["x4", place])
                value = scalars[SCALE + target] * (zero + mix * (one + mix * (two + mix * thrice)))
                values.append(rest.rows(first, 16) + value)
                Plane(last, target, place - 4).put(first, values[-1])
            Plane(total, place - 4).put(first, mixed(scalars, WEIGHT, values))
    total[5] = jnp.zeros_like(total[5])
    for place in range(OUTER, OUTER + HALF):
        index = place - 4
        order = index - 1 + back * (HALF + 1 - 2 * index)
        for first in chunks(Plane(total, 0), 16):
            states = [Plane(last, target, index).rows(first, 16) for target in range(NODES)]
            local = mixed(scalars, WEIGHT, [cubed(state) for state in states])
            nearby, centre = around_place(total, index, first, 16)
            force = diffusion * (nearby - 6.0 * centre) + reaction * local
            value = Plane(begin, place).rows(first, 16) + time_step * force
            Plane(mine, order).put(first, states[0])
            Plane(swap, order).put(first, states[2])
            Plane(swap, order + HALF).put(first, value)
    swap[2 * HALF] = total[HALF]


def finished(copies):
    for copy in copies:
        copy.start()
    for copy in copies:
        copy.wait()


def own_half_kernel(scalars, mine, swap, state, end, sems):
    upper = (scalars[CORE] > 0.5).astype(jnp.int32)
    base = HALF * upper
    inner = pl.ds(HALF + upper, HALF - 1)
    finished([
        pltpu.make_async_copy(mine, state.at[pl.ds(base, HALF)], sems.at[0]),
        pltpu.make_async_copy(swap.at[inner], end.at[pl.ds(base + upper, HALF - 1)], sems.at[1]),
    ])


def other_half_kernel(scalars, swap, other, state_before, end_before, state, end, cut, sems):
    upper = (scalars[CORE] > 0.5).astype(jnp.int32)
    base, base_other = HALF * upper, HALF * (1 - upper)
    edge, edge_other = (HALF - 1) * (1 - upper), (HALF - 1) * upper
    inner = pl.ds(HALF + 1 - upper, HALF - 1)
    halves = [
        pltpu.make_async_copy(other.at[pl.ds(0, HALF)], state.at[pl.ds(base_other, HALF)], sems.at[0]),
        pltpu.make_async_copy(other.at[inner], end.at[pl.ds(base_other + 1 - upper, HALF - 1)], sems.at[1]),
    ]
    for copy in halves:
        copy.start()
    cut[0] = swap[HALF + edge] + (time_step * diffusion) * other[2 * HALF]
    cut[1] = other[HALF + edge_other] + (time_step * diffusion) * swap[2 * HALF]
    finished([
        pltpu.make_async_copy(cut.at[0], end.at[base + edge], sems.at[2]),
        pltpu.make_async_copy(cut.at[1], end.at[base_other + edge_other], sems.at[3]),
    ])
    for copy in halves:
        copy.wait()


def join_call(scalars, mine, swap, other, shape):
    def placed(kernel, operands, before, scratch, sems):
        vmem, anywhere = pl.BlockSpec(memory_space=pltpu.VMEM), pl.BlockSpec(memory_space=pl.ANY)
        first = 1 + len(operands)
        return pl.pallas_call(
            kernel,
            out_shape=[jax.ShapeDtypeStruct(shape, F32)] * 2,
            in_specs=[pl.BlockSpec(memory_space=pltpu.SMEM)] + [vmem] * len(operands) + [anywhere] * len(before),
            out_specs=[anywhere] * 2,
            input_output_aliases={first + index: index for index in range(len(before))},
            scratch_shapes=[*scratch, pltpu.SemaphoreType.DMA((sems,))],
            compiler_params=pltpu.CompilerParams(vmem_limit_bytes=16 << 20),
            cost_estimate=pl.CostEstimate(flops=1000, bytes_accessed=1000, transcendentals=0),
        )(scalars, *operands, *before)

    halves = placed(own_half_kernel, [mine, swap], [], [], 2)
    return placed(other_half_kernel, [swap, other], halves, [pltpu.VMEM((2, *shape[1:]), F32)], 4)


def call(kernel, scalars, operands, outs, scratch, limit):
    return pl.pallas_call(
        kernel,
        out_shape=[jax.ShapeDtypeStruct(shape, F32) for shape in outs],
        in_specs=[pl.BlockSpec(memory_space=pltpu.SMEM)] + [pl.BlockSpec(memory_space=pltpu.VMEM)] * len(operands),
        out_specs=[pl.BlockSpec(memory_space=pltpu.VMEM)] * len(outs),
        scratch_shapes=[pltpu.VMEM(shape, F32) for shape in scratch],
        compiler_params=pltpu.CompilerParams(vmem_limit_bytes=limit << 20),
        cost_estimate=pl.CostEstimate(flops=1000, bytes_accessed=1000, transcendentals=0),
    )(scalars, *operands)


def on_device(start_old, nodes_old):
    slabs, slices = lax.axis_size("space"), lax.axis_size("tm")
    node_index = lax.axis_index("node")
    slice_index = lax.axis_index("tm")
    state, start = nodes_old[0, 0], start_old[0]
    slab, rows, columns = state.shape
    scalars = jnp.asarray(scalar_table())[node_index]
    scalars = scalars.at[FIRST].set((slice_index == 0).astype(F32))

    def after(array, other):
        return lax.optimization_barrier((array, other))[0]

    def planes(*lead):
        return (*lead, rows, columns)

    def across(array):
        return lax.ppermute(array, "node", [(node, node ^ 2) for node in range(NODES)])

    def beside(array):
        return lax.ppermute(array, "node", [(node, node ^ 1) for node in range(NODES)])

    always = scalars[WEIGHT] > 0.0

    def swapped(array):
        return lax.cond(always, beside, lambda array: array, array)

    def device(slab_, node, slice_):
        return ((slab_ % slabs) * NODES + node) * slices + slice_

    def spread(array, steps, by, flip=0):
        pairs = [
            (device(slab_, node, here), device(slab_ + by[node % 2], node ^ flip, there))
            for slab_ in range(slabs) for node in range(NODES) for here, there in steps
        ]
        return lax.ppermute(array, ("space", "node", "tm"), pairs)

    same = [(slice_, slice_) for slice_ in range(slices)]
    onward = [(slice_, slice_ + 1) for slice_ in range(slices - 1)]

    beside_state = beside(state)
    across_state = across(state)
    send_a, send_b = call(send_kernel, scalars, [state, beside_state], [planes(6), planes(4)], [], 16)
    halo_a = spread(send_a, same, (1, -1))
    halo_b = spread(send_b, same, (1, -1))
    corner_state = swapped(after(across_state, send_a))
    sources = [state, across_state, beside_state, corner_state]
    first_start = lax.dynamic_slice_in_dim(start, HALF * (1 - lax.rem(node_index, 2)), HALF, axis=0)
    passing_start = spread(first_start, [(0, 1)], (0, 0))
    (send_end,) = call(
        end_kernel, scalars, [*sources, after(start, passing_start)], [planes(5)], [planes(HALF + 2)], 16
    )
    near = spread(send_end, onward, (0, 0))
    away = spread(send_end, onward, (-1, 1), 1)
    across_a = across(after(halo_a, corner_state))
    halo_start = spread(passing_start, [(1, 0)], (1, -1))

    def stage(index, kernel, operands, limit):
        shapes = [planes(NODES, len(keys)) for keys in (kept_keys(index), spare_keys(index))]
        return call(kernel, scalars, operands, shapes[:1], shapes[1:], limit)[0]

    kept = stage(0, first_kernel, sources, 24)
    across_b = across(after(halo_b, kept))
    kept = stage(1, second_kernel, [*sources, halo_a, across_a, kept], 24)
    part = stage(2, third_kernel, [halo_a, across_a, halo_b, across_b, kept], 24)
    far = beside(after(near, part)[2:])
    mine, swap = call(
        last_kernel, scalars, [start, halo_start, near, far, away, kept, part], [planes(HALF), planes(2 * HALF + 1)],
        [planes(12), planes(11), planes(10), planes(NODES, 5), planes(6)], 24,
    )
    state_new, end_new = join_call(scalars, mine, swap, beside(swap), planes(slab))
    return (state_new[None, None], end_new[None])


def solution(mesh):
    return jax.shard_map(
        on_device,
        mesh=mesh,
        in_specs=(P("tm", "space", None, None), P("tm", "node", "space", None, None)),
        out_specs=(P("tm", "node", "space", None, None), P("tm", "space", None, None)),
        check_vma=False,
    )
```

```python
import functools

import jax
import jax.numpy as jnp
import numpy as np
from jax import lax
from jax.experimental import pallas as pl
from jax.experimental.pallas import tpu as pltpu
from jax.sharding import PartitionSpec as P

NODES = 4
PASSES = 4

time_step = 0.25
diffusion = 4.0
reaction = 1.0

F32 = jnp.float32

OUTER = 5
SLAB = 8
HALF = 4
RIGHT_ROWS, PASS_ROWS = 16, 32


def collocation(count):
    points = [-0.8611363115940526, -0.3399810435848563, 0.3399810435848563, 0.8611363115940526]
    raw_weights = [0.3478548451374538, 0.6521451548625461, 0.6521451548625461, 0.3478548451374538]
    node_times = [(point + 1.0) / 2.0 for point in points]
    quadrature = [[0.0 for column in range(count)] for target in range(count)]
    for source in range(count):
        coeffs = [1.0]
        scaling = 1.0
        for other in range(count):
            if other != source:
                other_time = node_times[other]
                shifted = [0.0] + coeffs
                for power in range(len(coeffs)):
                    shifted[power] = shifted[power] - other_time * coeffs[power]
                coeffs = shifted
                scaling = scaling * (node_times[source] - other_time)
        for target in range(count):
            target_time = node_times[target]
            integral = 0.0
            for power in range(len(coeffs)):
                integral = integral + coeffs[power] * target_time ** (power + 1) / (power + 1)
            quadrature[target][source] = integral / scaling
    return (node_times, quadrature, [weight / 2.0 for weight in raw_weights])


LIN, CUB, WEIGHT, MIX, SCALE, FIRST, CORE, COUNT = 0, 16, 32, 36, 40, 44, 45, 46


def scalar_table():
    times, quad, weights = collocation(NODES)
    table = np.zeros((NODES, COUNT), np.float64)
    for node in range(NODES):
        order = [node, node ^ 2, node ^ 1, node ^ 3]
        for place, target in enumerate(order):
            implicit = time_step * diffusion * times[target]
            scale = 1.0 / (1.0 + 6.0 * implicit)
            for index, source in enumerate(order):
                lin = time_step * diffusion * quad[target][source] - (implicit if source == target else 0.0)
                table[node, LIN + 4 * place + index] = scale * lin
                table[node, CUB + 4 * place + index] = scale * time_step * reaction * quad[target][source]
            table[node, WEIGHT + place] = weights[target]
            table[node, MIX + place] = scale * implicit
            table[node, SCALE + place] = scale
        table[node, CORE] = node & 1
    return table.astype(np.float32)


class Plane:
    def __init__(self, ref, *index):
        self.ref, self.index = ref, index

    def rows(self, first, count):
        return self.ref[(*self.index, pl.ds(first, count))]

    def put(self, first, value):
        self.ref[(*self.index, pl.ds(first, value.shape[0]))] = value


def flat_sum(plane, first, count):
    whole = plane.ref.shape[-2]
    centre = plane.rows(first, count)
    above, below = plane.rows((first - 8) % whole, 8), plane.rows((first + count) % whole, 8)
    longer = jnp.concatenate([above, centre, below], axis=0)
    vertical = pltpu.roll(longer, 1, 0)[8 : 8 + count] + pltpu.roll(longer, count + 15, 0)[8 : 8 + count]
    columns = centre.shape[1]
    return vertical + (pltpu.roll(centre, 1, 1) + pltpu.roll(centre, columns - 1, 1)), centre


def around(outside, plane, inside, first, count):
    flat, centre = flat_sum(plane, first, count)
    return (outside.rows(first, count) + inside.rows(first, count)) + flat, centre


def chunks(plane, count):
    return range(0, plane.ref.shape[-2], count)


def mixed(scalars, base, planes):
    own, across, beside, corner = (scalars[base + index] * plane for index, plane in enumerate(planes))
    return (own + across) + (beside + corner)


def cubed(state):
    return state - state * state * state


def counter(scalars):
    upper = (scalars[CORE] > 0.5).astype(jnp.int32)
    base, sign = upper * (SLAB - 1), 1 - 2 * upper
    return lambda place: base + sign * (place - OUTER)


def send_kernel(scalars, own, beside, halo_a, halo_b):
    plane = counter(scalars)
    for number, source in enumerate((own, beside)):
        for index in range(3):
            halo_a[index + 3 * number] = source[plane(10 + index)]
        for index in range(2):
            halo_b[index + 2 * number] = source[plane(8 + index)]


def end_kernel(scalars, own, across, beside, corner_far, start, out, total, corner, sem):
    plane = counter(scalars)
    sources = (own, across, beside, corner)
    weighted = [Plane(total, index) for index in range(HALF + 2)]
    fetch = pltpu.make_async_copy(corner_far, corner, sem.at[0])
    fetch.start()

    def states(place, first):
        return [Plane(source, plane(place)).rows(first, 32) for source in sources]

    for first in chunks(weighted[0], 32):
        weighted[0].put(first, jnp.zeros_like(weighted[0].rows(first, 32)))
    fetch.wait()
    for first in chunks(weighted[0], 32):
        for index in range(1, HALF + 2):
            value = mixed(scalars, WEIGHT, states(index + 4, first))
            weighted[index].put(first, value)
            if index == 1:
                Plane(out, 0).put(first, (time_step * diffusion) * value)
    for index in range(1, HALF + 1):
        place = index + 4
        for first in chunks(weighted[0], 32):
            local = mixed(scalars, WEIGHT, [cubed(state) for state in states(place, first)])
            nearby, centre = around(*weighted[index - 1 : index + 2], first, 32)
            force = diffusion * (nearby - 6.0 * centre) + reaction * local
            Plane(out, index).put(first, Plane(start, plane(place)).rows(first, 32) + time_step * force)


NAMES = ("g", "x1", "x2", "x3", "x4")
STAGES = [
    {"g": range(6, 12), "x1": range(6, 12), "x2": range(7, 11), "x3": range(8, 10), "x4": ()},
    {"g": range(3, 6), "x1": range(3, 6), "x2": range(4, 7), "x3": range(5, 8), "x4": range(6, 9)},
    {"g": range(1, 3), "x1": range(1, 3), "x2": range(2, 4), "x3": range(3, 5), "x4": range(4, 6)},
]
KEPT = [
    {"g": (6, 7, 8), "x1": (6, 7), "x2": (7, 8), "x3": (8, 9), "x4": ()},
    {"g": (3, 4, 5), "x1": (3, 4), "x2": (4, 5), "x3": (5, 6), "x4": (6, 7, 8)},
    {"g": (), "x1": (), "x2": (), "x3": (), "x4": (4, 5)},
]


def kept_keys(stage):
    return [(name, place) for name in NAMES for place in KEPT[stage][name]]


def spare_keys(stage):
    return [(name, place) for name in NAMES for place in STAGES[stage][name] if place not in KEPT[stage][name]]


def run_stage(stage, scalars, state, old, out, spare):
    where = {}
    for ref, keys in ((old, kept_keys(stage - 1) if stage else []), (out, kept_keys(stage)), (spare, spare_keys(stage))):
        where.update({key: (ref, index) for index, key in enumerate(keys)})

    def plane(name, target, place):
        ref, index = where[name, place]
        return Plane(ref, target, index)

    targets = range(NODES)
    for place in STAGES[stage]["g"]:
        sources = [[state(source, place + by) for by in (-1, 0, 1)] for source in range(NODES)]
        for first in chunks(sources[0][0], RIGHT_ROWS):
            nearby, centre = zip(*(around(*planes, first, RIGHT_ROWS) for planes in sources))
            spread_ = [value - 6.0 * middle for value, middle in zip(nearby, centre)]
            local = [cubed(middle) for middle in centre]
            for target in targets:
                value = mixed(scalars, LIN + 4 * target, spread_) + mixed(scalars, CUB + 4 * target, local)
                plane("g", target, place).put(first, value)
                plane("x1", target, place).put(first, value + scalars[MIX + target] * nearby[target])
    for name, before in (("x2", "x1"), ("x3", "x2"), ("x4", "x3")):
        for place in STAGES[stage][name]:
            for target in targets:
                planes = [plane(before, target, place + by) for by in (-1, 0, 1)]
                base, sink = plane("g", target, place), plane(name, target, place)
                for first in chunks(sink, PASS_ROWS):
                    nearby, _ = around(*planes, first, PASS_ROWS)
                    sink.put(first, base.rows(first, PASS_ROWS) + scalars[MIX + target] * nearby)


def first_kernel(scalars, own, across, beside, corner, out, spare):
    plane = counter(scalars)
    sources = (own, across, beside, corner)
    run_stage(0, scalars, lambda source, place: Plane(sources[source], plane(place)), None, out, spare)


def halo_state(halo, halo_across, first, count):
    def state(source, place):
        ref = (halo, halo_across, halo, halo_across)[source]
        return Plane(ref, (count if source >= 2 else 0) + place - first)

    return state


def second_kernel(scalars, own, across, beside, corner, halo_a, across_a, kept, out, spare):
    plane = counter(scalars)
    sources = (own, across, beside, corner)
    outer = halo_state(halo_a, across_a, 2, 3)

    def state(source, place):
        return outer(source, place) if place < OUTER else Plane(sources[source], plane(place))

    run_stage(1, scalars, state, kept, out, spare)


def third_kernel(scalars, halo_a, across_a, halo_b, across_b, kept, out, spare):
    inner, outer = halo_state(halo_a, across_a, 2, 3), halo_state(halo_b, across_b, 0, 2)

    def state(source, place):
        return outer(source, place) if place < 2 else inner(source, place)

    run_stage(2, scalars, state, kept, out, spare)


def last_kernel(scalars, start, halo_start, near, far, away, kept, part, mine, swap, begin, once, twice, last, total):
    plane = counter(scalars)
    begin_first = scalars[FIRST]
    back = (scalars[CORE] > 0.5).astype(jnp.int32)
    for place in range(1, 5):
        begin[place] = halo_start[place - 1 + back * (5 - 2 * place)] + away[5 - place]
    begin[4] = begin[4] + near[0]
    begin[5] = (begin_first * start[plane(5)] + near[1]) + away[0]
    for place in range(6, 9):
        begin[place] = begin_first * start[plane(place)] + near[place - 4]
    for place in range(9, 12):
        begin[place] = begin_first * start[plane(place)] + far[11 - place]

    def around_place(ref, place, first, count):
        return around(*(Plane(ref, place + by) for by in (-1, 0, 1)), first, count)

    for source, sink, places in ((begin, once, range(2, 11)), (once, twice, range(3, 10))):
        for place in places:
            out = Plane(sink, place)
            for first in chunks(out, 32):
                out.put(first, around_place(source, place, first, 32)[0])
    kept_x4 = {key: index for index, key in enumerate(kept_keys(1))}
    for place in range(4, 9):
        for first in chunks(Plane(total, 0), 16):
            thrice, two = around_place(twice, place, first, 16)
            zero, one = Plane(begin, place).rows(first, 16), Plane(once, place).rows(first, 16)
            values = []
            for target in range(NODES):
                mix = scalars[MIX + target]
                rest = Plane(part, target, place - 4) if place < 6 else Plane(kept, target, kept_x4["x4", place])
                value = scalars[SCALE + target] * (zero + mix * (one + mix * (two + mix * thrice)))
                values.append(rest.rows(first, 16) + value)
                Plane(last, target, place - 4).put(first, values[-1])
            Plane(total, place - 4).put(first, mixed(scalars, WEIGHT, values))
    total[5] = jnp.zeros_like(total[5])
    for place in range(OUTER, OUTER + HALF):
        index = place - 4
        for first in chunks(Plane(total, 0), 16):
            states = [Plane(last, target, index).rows(first, 16) for target in range(NODES)]
            local = mixed(scalars, WEIGHT, [cubed(state) for state in states])
            nearby, centre = around_place(total, index, first, 16)
            force = diffusion * (nearby - 6.0 * centre) + reaction * local
            value = Plane(begin, place).rows(first, 16) + time_step * force
            for sink, state in ((mine, states[0]), (swap, states[2])):
                Plane(sink, index - 1).put(first, state)
                Plane(sink, index - 1 + HALF).put(first, value)
    mine[2 * HALF] = total[HALF]
    swap[2 * HALF] = total[HALF]


def join_kernel(scalars, mine, other, state, end):
    plane = counter(scalars)
    for index in range(HALF):
        near, far = plane(OUTER + index), plane(OUTER + SLAB - 1 - index)
        state[near] = mine[index]
        state[far] = other[index]
        own, others = mine[HALF + index], other[HALF + index]
        if index == HALF - 1:
            own = own + (time_step * diffusion) * other[2 * HALF]
            others = others + (time_step * diffusion) * mine[2 * HALF]
        end[near] = own
        end[far] = others


def call(kernel, scalars, operands, outs, scratch, limit, far=None, sems=()):
    return pl.pallas_call(
        kernel,
        out_shape=[jax.ShapeDtypeStruct(shape, F32) for shape in outs],
        in_specs=[pl.BlockSpec(memory_space=pltpu.SMEM)] + [
            pl.BlockSpec(memory_space=pl.ANY if index == far else pltpu.VMEM) for index in range(len(operands))
        ],
        out_specs=[pl.BlockSpec(memory_space=pltpu.VMEM)] * len(outs),
        scratch_shapes=[pltpu.VMEM(shape, F32) for shape in scratch] + list(sems),
        compiler_params=pltpu.CompilerParams(vmem_limit_bytes=limit << 20),
        cost_estimate=pl.CostEstimate(flops=1000, bytes_accessed=1000, transcendentals=0),
    )(scalars, *operands)


def on_device(start_old, nodes_old):
    slabs, slices = lax.axis_size("space"), lax.axis_size("tm")
    node_index = lax.axis_index("node")
    slice_index = lax.axis_index("tm")
    state, start = nodes_old[0, 0], start_old[0]
    slab, rows, columns = state.shape
    scalars = jnp.asarray(scalar_table())[node_index]
    scalars = scalars.at[FIRST].set((slice_index == 0).astype(F32))

    def after(array, other):
        return lax.optimization_barrier((array, other))[0]

    def planes(*lead):
        return (*lead, rows, columns)

    def across(array):
        return lax.ppermute(array, "node", [(node, node ^ 2) for node in range(NODES)])

    def beside(array):
        return lax.ppermute(array, "node", [(node, node ^ 1) for node in range(NODES)])

    always = scalars[WEIGHT] > 0.0

    def swapped(array):
        return lax.cond(always, beside, lambda array: array, array)

    def device(slab_, node, slice_):
        return ((slab_ % slabs) * NODES + node) * slices + slice_

    def spread(array, steps, by, flip=0):
        pairs = [
            (device(slab_, node, here), device(slab_ + by[node % 2], node ^ flip, there))
            for slab_ in range(slabs) for node in range(NODES) for here, there in steps
        ]
        return lax.ppermute(array, ("space", "node", "tm"), pairs)

    same = [(slice_, slice_) for slice_ in range(slices)]
    onward = [(slice_, slice_ + 1) for slice_ in range(slices - 1)]

    beside_state = beside(state)
    across_state = across(state)
    send_a, send_b = call(send_kernel, scalars, [state, beside_state], [planes(6), planes(4)], [], 16)
    halo_a = spread(send_a, same, (1, -1))
    halo_b = spread(send_b, same, (1, -1))
    corner_state = swapped(after(across_state, send_a))
    sources = [state, across_state, beside_state, corner_state]
    first_start = lax.dynamic_slice_in_dim(start, HALF * (1 - lax.rem(node_index, 2)), HALF, axis=0)
    passing_start = spread(first_start, [(0, 1)], (0, 0))
    (send_end,) = call(
        end_kernel, scalars, [*sources, after(start, passing_start)], [planes(5)], [planes(HALF + 2), planes(slab)], 16, 3,
        [pltpu.SemaphoreType.DMA((1,))],
    )
    near = spread(send_end, onward, (0, 0))
    away = spread(send_end, onward, (-1, 1), 1)
    across_a = across(after(halo_a, corner_state))
    halo_start = spread(passing_start, [(1, 0)], (1, -1))

    def stage(index, kernel, operands, limit):
        shapes = [planes(NODES, len(keys)) for keys in (kept_keys(index), spare_keys(index))]
        return call(kernel, scalars, operands, shapes[:1], shapes[1:], limit)[0]

    kept = stage(0, first_kernel, sources, 24)
    across_b = across(after(halo_b, kept))
    kept = stage(1, second_kernel, [*sources, halo_a, across_a, kept], 24)
    part = stage(2, third_kernel, [halo_a, across_a, halo_b, across_b, kept], 24)
    far = beside(after(near, part)[2:])
    mine, swap = call(
        last_kernel, scalars, [start, halo_start, near, far, away, kept, part], [planes(2 * HALF + 1)] * 2,
        [planes(12), planes(11), planes(10), planes(NODES, 5), planes(6)], 24,
    )
    state_new, end_new = call(join_kernel, scalars, [mine, beside(swap)], [planes(slab)] * 2, [], 16)
    return (state_new[None, None], end_new[None])


def solution(mesh):
    return jax.shard_map(
        on_device,
        mesh=mesh,
        in_specs=(P("tm", "space", None, None), P("tm", "node", "space", None, None)),
        out_specs=(P("tm", "node", "space", None, None), P("tm", "space", None, None)),
        check_vma=False,
    )
```
